32 devices in a mesh: shot: 4 (over x, core), space: 8 (over z, y).
Axes of the slice: x: 2, y: 2, z: 4, core: 2. Of those that a mesh axis runs over, the one named last changes fastest.
Arguments:
- residual_traces: float32 [4, 12, 2048], P('shot', None, 'space'), may hold values from -6 to 6
- owners: int32 [4, 2048, 1], P('shot', 'space'), may hold values from 0 to 7; in each aligned block of 256 rows (0 to 255, 256 to 511, ..., all dimensions but the last counted through in order) at most 64 rows name the same one
- surface_cells: int32 [4, 2048], P('shot', 'space'), may hold values from 0 to 511
- trace_counts: int32 [4], P('shot'), may hold values from 512 to 2048, as said below
- start_current: float32 [4, 64, 64, 256], P('shot', 'space'), may hold values from -6 to 6
- start_later: float32 [4, 64, 64, 256], P('shot', 'space'), may hold values from -6 to 6
- forward_accel: bfloat16 [4, 12, 64, 64, 256], P('shot', None, 'space'), may hold values from -6 to 6
- courant_sq: float32 [64, 64, 256], P('space'), may hold values from 0.04 to 0.16
Outputs:
- adjoint_field: float32 [4, 64, 64, 256], P('shot', 'space')
- velocity_grad: float32 [64, 64, 256], P('space', 'shot')
The draws below stay inside these ranges and needn't reach their ends.
Inputs may be any that keep to these rules, and one draw needn't show every extreme that they name: `owners`: among the receivers of one device, no subdomain is named more than 64 times. `trace_counts`: some shot has all 2048 traces live.
All inputs are finite; a program needn't handle non-finite values.
Results may differ from the reference program's by a relative error of at most 0.0003.
Values sent between devices are 32-bit elements; how exact they have to be, the bound alone decides.
No kernel may reach another device: no remote copies, remote signals or barrier semaphores. Data moves between devices by JAX's collectives and lax.ppermute only.
A program may use at most 64 MiB of HBM per device.

```python
import math
import jax
import jax.numpy as jnp
import numpy as np
from jax import lax

CX = 8
CY = 64
STEPS = 12
RECV_DEV = 256
CAP = 64
NSHOTS = 4
NX = 64
NY = 64
NZ = 256
RECV = 2048
N_SPACE = 8


def draw_trace_counts(key, part):
    first_key, second_key = jax.random.split(jax.random.fold_in(key, 17))
    values = jax.random.randint(first_key, (NSHOTS,), RECV // 4, RECV + 1)
    full_shot = jax.random.randint(second_key, (), 0, NSHOTS)
    return jnp.where(jnp.arange(NSHOTS) == full_shot, RECV, values).astype(jnp.int32)


def touch_ends(entries, own_key, smallest, largest):
    spot = [jax.random.randint(jax.random.fold_in(own_key, axis), (), 0, length) for axis, length in enumerate(entries.shape)]
    longest = entries.shape.index(max(entries.shape))
    beside = spot[:longest] + [(spot[longest] + 1) % entries.shape[longest]] + spot[longest + 1:]
    return entries.at[tuple(spot)].set(smallest).at[tuple(beside)].set(largest)


def block_scale(stream_key, shape, shards, smallest, top_value):
    gain = 1.0
    for axis_at, blocks in shards:
        draws = jax.random.uniform(jax.random.fold_in(jax.random.fold_in(stream_key, 6), axis_at), (blocks,), jnp.float32, smallest / len(shards), top_value / len(shards))
        gain = gain * jnp.repeat(jnp.exp(draws), shape[axis_at] // blocks).reshape((-1,) + (1,) * (len(shape) - 1 - axis_at))
    return gain


def shared_out(key, own, number, rows, number_of, top, limit, lean):
    sequence = jax.random.permutation(key, number_of)
    crowded, usual = shares(number_of, rows * top, limit, lean, True), shares(number_of, rows * top, limit, lean, False)
    places = jnp.arange(number_of)

    def named(sizes, turn):
        used = int((sizes > 0).sum())
        fixed = max(1, used // 4)
        passed = fixed + (places - fixed + turn * (used - fixed)) % max(1, number_of - fixed)
        return jnp.zeros((number_of,), jnp.int32).at[sequence[jnp.where(places < fixed, places, passed)]].set(jnp.asarray(sizes, jnp.int32))

    sizes = jnp.where(number % 4 == 0, named(crowded, number // 4), named(usual, number - number // 4 - 1))
    mixed = jax.random.permutation(jax.random.fold_in(own, 3), number_of)
    giver, sink = mixed[0:number_of // 2 * 2:2], mixed[1:number_of // 2 * 2:2]
    room = jnp.minimum(sizes[giver] - 1, limit - sizes[sink]) // 2
    room = jnp.where((giver == sequence[0]) | (sink == sequence[0]) | (sizes[sink] == 0), 0, jnp.maximum(room, 0))
    passed = jax.random.randint(jax.random.fold_in(own, 4), (number_of // 2,), 0, 1 << 20) % (room + 1)
    sizes = sizes.at[giver].add(-passed).at[sink].add(passed)
    labels = jnp.searchsorted(jnp.cumsum(sizes), jnp.arange(rows * top), side="right").astype(jnp.int32)
    listing = labels.reshape(top, rows).T
    listing = listing[jax.random.permutation(jax.random.fold_in(own, 1), rows)]
    turn = jax.random.randint(jax.random.fold_in(own, 2), (rows, 1), 0, top)
    return jnp.take_along_axis(listing, (jnp.arange(top)[None, :] + turn) % top, axis=1)


def shares(number_of, total, reach, slope, full):
    portions = [(1 << 20) // math.isqrt(rank ** slope) + 1 for rank in range(1, number_of + 1)]
    largest = reach if full else min(reach, max(-(-total // number_of), total * portions[0] // sum(portions)))
    least = 1 if total - largest >= number_of - 1 else 0
    counts, surplus = [largest] + [least] * (number_of - 1), total - largest - least * (number_of - 1)
    while surplus > 0:
        movable = [i for i in range(1, number_of) if counts[i] < largest] or [i for i in range(1, number_of) if counts[i] < reach]
        mass, remaining = sum([portions[i] for i in movable]), surplus
        for i in movable:
            addition = min(reach - counts[i], max(1, remaining * portions[i] // mass), surplus)
            counts[i] = counts[i] + addition
            surplus = surplus - addition
    return np.array(counts)


def scatter_about(rng, extent, width, bound, shards=(), kind=jnp.bfloat16):
    level = block_scale(rng, extent, shards, -0.22, 0.18) if shards else 1.0
    entries = jax.random.normal(rng, extent, jnp.float32) * width * level
    return jnp.minimum(jnp.maximum(entries, -bound), bound).astype(kind)


def setup_inputs(seed: int = 0) -> dict:
    key_list = jax.random.split(jax.random.key(seed), 9)
    residual_traces = scatter_about(key_list[0], (NSHOTS, STEPS, RECV), 1.0, 6.0, ((0, 4), (2, 8)), jnp.float32)
    owners_keys = jax.random.split(jax.random.fold_in(key_list[1], 1), NSHOTS * RECV // RECV_DEV)
    owners_turns = jax.random.permutation(jax.random.fold_in(key_list[1], 3), NSHOTS * RECV // RECV_DEV)
    owners = jax.vmap(lambda own, number: shared_out(jax.random.fold_in(key_list[1], 2), own, number, RECV_DEV, N_SPACE, 1, CAP, 2))(owners_keys, owners_turns).reshape((NSHOTS, RECV, 1))
    surface_cells = touch_ends(jax.random.randint(key_list[2], (NSHOTS, RECV), 0, CX * CY), jax.random.fold_in(key_list[2], 1), 0, (CX * CY) - 1).astype(jnp.int32)
    trace_counts = draw_trace_counts(jax.random.fold_in(key_list[8], 71), 0)
    start_current = scatter_about(key_list[4], (NSHOTS, NX, NY, NZ), 1.0, 6.0, ((0, 4), (1, 8)), jnp.float32)
    start_later = scatter_about(key_list[5], (NSHOTS, NX, NY, NZ), 1.0, 6.0, ((0, 4), (1, 8)), jnp.float32)
    forward_accel = scatter_about(key_list[6], (NSHOTS, STEPS, NX, NY, NZ), 1.0, 6.0, ((0, 4), (2, 8)))
    courant_sq = jnp.clip(jnp.exp(math.log(0.16) - 1.3862944 * jax.random.uniform(key_list[7], (NX, NY, NZ), jnp.float32) ** block_scale(key_list[7], (NX, NY, NZ), ((0, 8),), -0.2, 0.2)), 0.04, 0.16)
    return {"residual_traces": residual_traces, "owners": owners, "surface_cells": surface_cells, "trace_counts": trace_counts, "start_current": start_current, "start_later": start_later, "forward_accel": forward_accel, "courant_sq": courant_sq}


STENCIL_WEIGHTS = (-205.0 / 72.0, 8.0 / 5.0, -1.0 / 5.0, 8.0 / 315.0, -1.0 / 560.0)


def laplace(padded):
    length = padded.shape[0] - 8
    across = padded.shape[1] - 8
    height = padded.shape[2] - 8

    def window(off_x, off_y, off_z):
        return lax.slice(padded, (4 + off_x, 4 + off_y, 4 + off_z),
                         (4 + off_x + length, 4 + off_y + across, 4 + off_z + height))

    summed = (3.0 * STENCIL_WEIGHTS[0]) * window(0, 0, 0)
    for offset in range(1, 5):
        six_taps = window(offset, 0, 0) + window(-offset, 0, 0) + window(0, offset, 0)
        six_taps = six_taps + window(0, -offset, 0) + window(0, 0, offset) + window(0, 0, -offset)
        summed = summed + STENCIL_WEIGHTS[offset] * six_taps
    return summed


def one_shot(traces, owners, surface, live_count, first_field, prior_field, forward, courant_sq):
    number = jnp.arange(traces.shape[1], dtype=jnp.int32)
    weights = jnp.where((number < live_count)[None, :], traces, jnp.zeros_like(traces))
    row_x = owners[:, 0] * CX + surface // CY
    col_y = surface % CY
    planes = jnp.zeros((STEPS, NX, NY), jnp.float32).at[:, row_x, col_y].add(weights)
    current = first_field
    later = prior_field
    gradient = jnp.zeros((NX, NY, NZ), jnp.float32)
    for section in range(STEPS):
        fresh = 2.0 * current - later + courant_sq * laplace(jnp.pad(current, 4))
        fresh = fresh.at[:, :, 2].add(planes[section])
        gradient = gradient + fresh * forward[section].astype(jnp.float32)
        later, current = current, fresh
    return current, gradient


def reference(residual_traces, owners, surface_cells, trace_counts, start_current, start_later,
              forward_accel, courant_sq):
    fields = []
    gradients = []
    for shot_num in range(NSHOTS):
        current, gradient = one_shot(residual_traces[shot_num], owners[shot_num], surface_cells[shot_num],
                                     trace_counts[shot_num], start_current[shot_num], start_later[shot_num],
                                     forward_accel[shot_num], courant_sq)
        fields.append(current)
        gradients.append(gradient)
    summed = gradients[0]
    for extra in gradients[1:]:
        summed = summed + extra
    return jnp.stack(fields), summed
```

```python
import functools

import jax
import jax.numpy as jnp
from jax import lax
from jax.experimental import pallas as pl
from jax.experimental.pallas import tpu as pltpu
from jax.sharding import PartitionSpec as P

SCALE = 5040.0
TAPS = (8064.0, -1008.0, 128.0, -9.0)
CENTRE = 3.0 * (-205.0 / 72.0)

LIMIT = 40 * 1024 * 1024
VM = pltpu.VMEM
F32 = jnp.float32
BF16 = jnp.bfloat16


def vmem(x):
    return pltpu.with_memory_space_constraint(x, VM)


def band(rows, cols, block):
    r = lax.broadcasted_iota(jnp.int32, (rows, cols), 0)
    c = lax.broadcasted_iota(jnp.int32, (rows, cols), 1)
    r = r % cols
    c = c % rows
    gap = jnp.abs(r - c)
    out = jnp.zeros((rows, cols), F32)
    for j, w in enumerate(TAPS):
        out = jnp.where(gap == j + 1, w, out)
    return jnp.where(r // block == c // block, out, 0.0).astype(BF16)


def advance(src, so, prev, po, dst, do, a_ref, c_ref, q_ref, wz_ref, wy_ref, start, groups, k, extra=None):
    ny, nz = src.shape[1], src.shape[2]
    half = q_ref.shape[2]
    lane = lax.broadcasted_iota(jnp.int32, (ny, half), 1)
    for g in range(groups):
        t = start + 4 * g
        v = src[t + so : t + so + 4].reshape(4 * ny, nz)
        hi = v.astype(BF16)
        lo = (v - hi.astype(F32)).astype(BF16)
        s = jnp.dot(jnp.concatenate([hi, lo], 1), wz_ref[...], preferred_element_type=F32)
        s = s + jnp.dot(wy_ref[...], jnp.concatenate([hi, lo], 0), preferred_element_type=F32)
        for i in range(4):
            p = t + i
            total = s[i * ny : (i + 1) * ny]
            for j, w in enumerate(TAPS):
                total = total + w * (src[p + so + j + 1] + src[p + so - j - 1])
            fresh = a_ref[p + 4] * src[p + so] - prev[p + po] + c_ref[p + 4] * total
            x = p + 4
            shift = (2 - ((x % 8) * 16 + k)) % half
            q = q_ref[x // 8]
            q = jnp.where(lane == 2, pltpu.roll(q, shift, 1), 0.0)
            fresh = jnp.concatenate([fresh[:, :half] + q, fresh[:, half:]], 1)
            dst[p + do] = fresh
            if extra is not None:
                extra[p - start] = fresh


def local_of(scal_ref, y, p, length):
    g = y * length + p
    odd = scal_ref[1]
    return jnp.where(odd == 1, 2 * length - 1 - g, g)


def q_kernel(scal_ref, gathered_ref, q_ref, *, steps, length):
    n, rows, width = gathered_ref.shape
    across = q_ref.shape[1]
    level, odd = scal_ref[0], scal_ref[1]
    x_iota = lax.broadcasted_iota(jnp.int32, (8, 16, width), 0)
    y_iota = lax.broadcasted_iota(jnp.int32, (across, width), 0)

    def body(b, acc):
        block = gathered_ref[b]
        code = block[steps : steps + 1].astype(jnp.int32)
        gx = code // across
        y = code - gx * across
        gx = gx - level * (2 * length)
        x = jnp.where(odd == 1, 2 * length - 1 - gx, gx) + 4
        one_y = jnp.where(y_iota == y, 1.0, 0.0).astype(BF16)
        out = []
        for j in range(3):
            t = jnp.where(x_iota + 8 * j == x[None], block[None], 0.0).reshape(8 * 16, width)
            hi = t.astype(BF16)
            lo = (t - hi.astype(F32)).astype(BF16)
            dims = (((1,), (1,)), ((), ()))
            o = lax.dot_general(one_y, hi, dims, preferred_element_type=F32)
            o = o + lax.dot_general(one_y, lo, dims, preferred_element_type=F32)
            out.append(acc[j] + o)
        return tuple(out)

    zero = jnp.zeros(q_ref.shape[1:], F32)
    acc = lax.fori_loop(0, n, body, (zero, zero, zero))
    for j in range(3):
        q_ref[j] = acc[j]


def init_kernel(scal_ref, cur_own, cur_oth, lat_own, lat_oth, c_own, c_oth,
                e_ref, o_ref, a_ref, c_ref, wz_ref, wy_ref, send_a, send_b):
    length, ny, nz = cur_own.shape
    y = scal_ref[2]
    for p in range(length):
        for who, cur, lat, cou in ((y, cur_own, lat_own, c_own), (1 - y, cur_oth, lat_oth, c_oth)):
            j = local_of(scal_ref, who, p, length)
            e_ref[j + 8] = cur[p]
            o_ref[j + 4] = lat[p]
            cv = cou[p]
            c_ref[j + 4] = cv * (1.0 / SCALE)
            a_ref[j + 4] = 2.0 + CENTRE * cv
    send_a[0:8] = e_ref[16:24]
    send_a[8:12] = o_ref[16:20]
    send_a[12:16] = c_ref[16:20]
    send_b[0:8] = e_ref[8:16]
    send_b[8:12] = o_ref[4:8]
    send_b[12:16] = c_ref[4:8]
    wz_ref[...] = band(2 * nz, nz, nz)
    wy_ref[...] = band(4 * ny, 8 * ny, ny)


def inner_kernel(scal_ref, e_ref, o_in, a_ref, c_ref, q_ref, wz_ref, wy_ref, f_ref, g_in, o_ref, g_ref, *, r, length):
    y = scal_ref[2]
    if r > 0:
        for p in range(length):
            j = local_of(scal_ref, y, p, length)
            add = o_ref[j + 4] * f_ref[2 * r - 2, p].astype(F32) + e_ref[j + 8] * f_ref[2 * r - 1, p].astype(F32)
            g_ref[p] = add if r == 1 else g_ref[p] + add
    advance(e_ref, 8, o_ref, 4, o_ref, 4, a_ref, c_ref, q_ref, wz_ref, wy_ref, 4, 2, 2 * r)


def side_kernel(recv, e_in, o_in, a_in, c_in, q_ref, wz_ref, wy_ref, *outs, r, side, first):
    if first:
        e_ref, o_ref, a_ref, c_ref, new = outs
    else:
        e_ref, o_ref, new = outs
        a_ref, c_ref = a_in, c_in
    for i in range(8):
        if side == "a":
            e_ref[24 + i] = recv[7 - i]
        else:
            e_ref[7 - i] = recv[i]
    if first:
        for i in range(4):
            if side == "a":
                to, at = 20 + i, 3 - i
            else:
                to, at = 3 - i, i
            o_ref[to] = recv[8 + at]
            cv = recv[12 + at]
            c_ref[to] = cv
            a_ref[to] = 2.0 + (CENTRE * SCALE) * cv
    args = (a_ref, c_ref, q_ref, wz_ref, wy_ref)
    advance(e_ref, 8, o_ref, 4, o_ref, 4, *args, 12 if side == "a" else -4, 2, 2 * r)
    advance(o_ref, 4, e_ref, 8, e_ref, 8, *args, 8 if side == "a" else 0, 2, 2 * r + 1, extra=new)


def final_kernel(scal_ref, e_ref, o_ref, f_ref, g_in, field_ref, g_ref, *, steps):
    length = field_ref.shape[0]
    y = scal_ref[2]
    for p in range(length):
        j = local_of(scal_ref, y, p, length)
        last = e_ref[j + 8]
        field_ref[p] = last
        g_ref[p] = g_in[p] + o_ref[j + 4] * f_ref[steps - 2, p].astype(F32) + last * f_ref[steps - 1, p].astype(F32)


def call(kernel, out_shapes, args, aliases=None, flops=0, name=None):
    smem = pl.BlockSpec(memory_space=pltpu.SMEM)
    vm = pl.BlockSpec(memory_space=VM)
    specs = [smem if a.dtype == jnp.int32 and a.ndim == 1 else vm for a in args]
    args = [a if s is smem else vmem(a) for a, s in zip(args, specs)]
    return pl.pallas_call(
        kernel,
        out_shape=out_shapes,
        in_specs=specs,
        out_specs=jax.tree.map(lambda _: vm, out_shapes),
        input_output_aliases=aliases or {},
        compiler_params=pltpu.CompilerParams(vmem_limit_bytes=LIMIT),
        cost_estimate=pl.CostEstimate(flops=flops, bytes_accessed=1 << 20, transcendentals=0),
        name=name,
    )(*args)


def shards(residual_traces, owners, surface_cells, trace_counts, start_current, start_later, forward_accel, courant_sq):
    traces = residual_traces[0]
    forward = forward_accel[0]
    cur, later = start_current[0], start_later[0]
    length, ny, nz = courant_sq.shape
    steps, width = traces.shape
    n = lax.axis_size("space")
    levels = n // 2
    me = lax.axis_index("space")
    level = me // 2
    scal = jnp.stack([level, level % 2, me % 2, me * 0]).astype(jnp.int32)

    def pairs(low_levels):
        out = []
        for lv in low_levels:
            for y in range(2):
                lo, hi = 2 * lv + y, 2 * lv + 2 + y
                out += [(lo, hi), (hi, lo)]
        return out

    swap_y = [(i, i ^ 1) for i in range(n)]
    swap_a = pairs(range(0, levels - 1, 2))
    swap_b = pairs(range(1, levels - 1, 2))

    number = me * width + jnp.arange(width, dtype=jnp.int32)
    live = jnp.where(number < trace_counts[0], 1.0, 0.0)
    code = (owners[0, :, 0] * (length * ny) + surface_cells[0]).astype(F32)
    payload = jnp.concatenate([traces * live[None], code[None], jnp.zeros((16 - steps - 1, width), F32)], 0)
    gathered = lax.all_gather(payload, "space", axis=0)

    cur_oth = lax.ppermute(cur, "space", swap_y)
    lat_oth = lax.ppermute(later, "space", swap_y)
    c_oth = lax.ppermute(courant_sq, "space", swap_y)

    plane = lambda k: VM((k, ny, nz), F32)
    e, o, a, c, wz, wy, send_a, send_b = call(
        init_kernel,
        [plane(32), plane(24), plane(24), plane(24), VM((2 * nz, nz), BF16), VM((4 * ny, 8 * ny), BF16),
         plane(16), plane(16)],
        [scal, cur, cur_oth, later, lat_oth, courant_sq, c_oth],
        name="init",
    )
    q = call(
        functools.partial(q_kernel, steps=steps, length=length),
        VM((3, ny, 128), F32),
        [scal, gathered],
        name="receivers",
    )
    g = None
    work = 2 * 16 * ny * nz * 60
    for r in range(steps // 2):
        recv_a = lax.ppermute(send_a, "space", swap_a)
        recv_b = lax.ppermute(send_b, "space", swap_b)
        if g is None:
            g = jnp.zeros((length, ny, nz), F32)
        o, g = call(
            functools.partial(inner_kernel, r=r, length=length),
            [plane(24), plane(length)],
            [scal, e, o, a, c, q, wz, wy, forward, g],
            {2: 0, 9: 1},
            flops=work,
            name=f"inner{r}",
        )
        for side in "ab":
            recv = recv_a if side == "a" else recv_b
            first = r == 0
            kern = functools.partial(side_kernel, r=r, side=side, first=first)
            if first:
                e, o, a, c, new = call(
                    kern, [plane(32), plane(24), plane(24), plane(24), plane(8)],
                    [recv, e, o, a, c, q, wz, wy], {1: 0, 2: 1, 3: 2, 4: 3}, flops=work, name=f"side_{side}{r}")
            else:
                e, o, new = call(
                    kern, [plane(32), plane(24), plane(8)],
                    [recv, e, o, a, c, q, wz, wy], {1: 0, 2: 1}, flops=work, name=f"side_{side}{r}")
            if side == "a":
                send_a = new
            else:
                send_b = new

    field, g = call(
        functools.partial(final_kernel, steps=steps),
        [plane(length), plane(length)],
        [scal, e, o, forward, g],
        name="final",
    )
    shot = lax.axis_index("shot")
    sx, sc = shot // 2, shot % 2
    part = ny // 4
    quarters = g.reshape(length, 2, 2, part, nz)
    give = lax.dynamic_index_in_dim(quarters, 1 - sc, 2, keepdims=False)
    keep = lax.dynamic_index_in_dim(quarters, sc, 2, keepdims=False)
    keep = keep + lax.ppermute(give, "shot", [(0, 1), (1, 0), (2, 3), (3, 2)])
    give = lax.dynamic_index_in_dim(keep, 1 - sx, 1, keepdims=False)
    mine = lax.dynamic_index_in_dim(keep, sx, 1, keepdims=False)
    grad = mine + lax.ppermute(give, "shot", [(0, 2), (2, 0), (1, 3), (3, 1)])
    return field[None], grad


def solution(mesh):
    placed = (
        P("shot", None, "space"),
        P("shot", "space", None),
        P("shot", "space"),
        P("shot"),
        P("shot", "space", None, None),
        P("shot", "space", None, None),
        P("shot", None, "space", None, None),
        P("space", None, None),
    )
    return jax.shard_map(
        shards,
        mesh=mesh,
        in_specs=placed,
        out_specs=(P("shot", "space", None, None), P("space", "shot", None)),
        check_vma=False,
    )
```

```python
import functools

import jax
import jax.numpy as jnp
from jax import lax
from jax.experimental import pallas as pl
from jax.experimental.pallas import tpu as pltpu
from jax.sharding import PartitionSpec as P

SCALE = 5040.0
TAPS = (8064.0, -1008.0, 128.0, -9.0)
CENTRE = 3.0 * (-205.0 / 72.0)

LIMIT = 8 * 1024 * 1024
VM = pltpu.VMEM
F32 = jnp.float32
BF16 = jnp.bfloat16


def vmem(x):
    return pltpu.with_memory_space_constraint(x, VM)


def band(rows, cols, block):
    r = lax.broadcasted_iota(jnp.int32, (rows, cols), 0)
    c = lax.broadcasted_iota(jnp.int32, (rows, cols), 1)
    r = r % cols
    c = c % rows
    gap = jnp.abs(r - c)
    out = jnp.zeros((rows, cols), F32)
    for j, w in enumerate(TAPS):
        out = jnp.where(gap == j + 1, w, out)
    return jnp.where(r // block == c // block, out, 0.0).astype(BF16)


def advance(src, so, prev, po, dst, do, a_ref, c_ref, q_ref, wz_ref, wy_ref, start, groups, k, extra=None):
    ny, nz = src.shape[1], src.shape[2]
    half = q_ref.shape[2]
    lane = lax.broadcasted_iota(jnp.int32, (ny, half), 1)
    for g in range(groups):
        t = start + 4 * g
        v = src[t + so : t + so + 4].reshape(4 * ny, nz)
        hi = v.astype(BF16)
        lo = (v - hi.astype(F32)).astype(BF16)
        s = jnp.dot(jnp.concatenate([hi, lo], 1), wz_ref[...], preferred_element_type=F32)
        s = s + jnp.dot(wy_ref[...], jnp.concatenate([hi, lo], 0), preferred_element_type=F32)
        for i in range(4):
            p = t + i
            total = s[i * ny : (i + 1) * ny]
            for j, w in enumerate(TAPS):
                total = total + w * (src[p + so + j + 1] + src[p + so - j - 1])
            fresh = a_ref[p + 4] * src[p + so] - prev[p + po] + c_ref[p + 4] * total
            x = p + 4
            shift = (2 - ((x % 8) * 16 + k)) % half
            q = q_ref[x // 8]
            q = jnp.where(lane == 2, pltpu.roll(q, shift, 1), 0.0)
            fresh = jnp.concatenate([fresh[:, :half] + q, fresh[:, half:]], 1)
            dst[p + do] = fresh
            if extra is not None:
                extra[p - start] = fresh


def local_of(scal_ref, g, length):
    return jnp.where(scal_ref[1] == 1, 2 * length - 1 - g, g)


def q_kernel(scal_ref, gathered_ref, q_ref, *, steps, length):
    n, rows, width = gathered_ref.shape
    across = q_ref.shape[1]
    level, odd = scal_ref[0], scal_ref[1]
    x_iota = lax.broadcasted_iota(jnp.int32, (8, 16, width), 0)
    y_iota = lax.broadcasted_iota(jnp.int32, (across, width), 0)

    def body(b, acc):
        block = gathered_ref[b]
        code = block[steps : steps + 1].astype(jnp.int32)
        gx = code // across
        y = code - gx * across
        gx = gx - level * (2 * length)
        x = jnp.where(odd == 1, 2 * length - 1 - gx, gx) + 4
        one_y = jnp.where(y_iota == y, 1.0, 0.0).astype(BF16)
        out = []
        for j in range(3):
            t = jnp.where(x_iota + 8 * j == x[None], block[None], 0.0).reshape(8 * 16, width)
            hi = t.astype(BF16)
            lo = (t - hi.astype(F32)).astype(BF16)
            dims = (((1,), (1,)), ((), ()))
            o = lax.dot_general(one_y, hi, dims, preferred_element_type=F32)
            o = o + lax.dot_general(one_y, lo, dims, preferred_element_type=F32)
            out.append(acc[j] + o)
        return tuple(out)

    zero = jnp.zeros(q_ref.shape[1:], F32)
    acc = lax.fori_loop(0, n, body, (zero, zero, zero))
    for j in range(3):
        q_ref[j] = acc[j]


def field_kernel(scal_ref, cur_own, cur_oth, lat_own, lat_edge, lat_rest, e_ref, o_ref, wz_ref, wy_ref):
    length, ny, nz = cur_own.shape
    half = length // 2
    y = scal_ref[2]
    for p in range(length):
        j = local_of(scal_ref, y * length + p, length)
        e_ref[j + 8] = cur_own[p]
        o_ref[j + 4] = lat_own[p]
        j = local_of(scal_ref, (1 - y) * length + p, length)
        e_ref[j + 8] = cur_oth[p]
    for p in range(half):
        j = local_of(scal_ref, (1 - y) * length + half * (1 - y) + p, length)
        o_ref[j + 4] = lat_edge[p]
        j = local_of(scal_ref, (1 - y) * length + half * y + p, length)
        o_ref[j + 4] = lat_rest[p]
    wz_ref[...] = band(2 * nz, nz, nz)
    wy_ref[...] = band(4 * ny, 8 * ny, ny)


def halo_at(scal_ref, upper, p, depth, length):
    g = jnp.where(upper == 1, 2 * length + p, p - depth)
    return local_of(scal_ref, g, length)


def model_kernel(scal_ref, c_own, c_oth, c_core, d_cur, d_edge, r_c, e_in, o_in, a_ref, c_ref, e_ref, o_ref):
    length = c_own.shape[0]
    half, two = length // 2, length // 4
    y, core = scal_ref[2], scal_ref[3]

    def put(j, cv):
        c_ref[j + 4] = cv * (1.0 / SCALE)
        a_ref[j + 4] = 2.0 + CENTRE * cv

    for p in range(length):
        put(local_of(scal_ref, y * length + p, length), c_own[p])
    base = (1 - y) * length
    for p in range(two):
        for who, piece, at in ((core, c_oth, 0), (1 - core, c_core, 0)):
            put(local_of(scal_ref, base + half * (1 - y) + two * who + p, length), piece[at + p])
            put(local_of(scal_ref, base + half * y + two * who + p, length), piece[at + two + p])
        put(halo_at(scal_ref, 1 - y, two * core + p, half, length), d_edge[half + p])
        put(halo_at(scal_ref, 1 - y, two * (1 - core) + p, half, length), c_core[half + p])
        put(halo_at(scal_ref, y, two * core + p, half, length), r_c[p])
        put(halo_at(scal_ref, y, two * (1 - core) + p, half, length), c_core[half + two + p])
    for p in range(length):
        e_ref[halo_at(scal_ref, 1 - y, p, length, length) + 8] = d_cur[p]
    for p in range(half):
        o_ref[halo_at(scal_ref, 1 - y, p, half, length) + 4] = d_edge[p]


def inner_kernel(scal_ref, e_ref, o_in, a_ref, c_ref, q_ref, wz_ref, wy_ref, f_ref, g_in, o_ref, g_ref, *, r, length):
    y = scal_ref[2]
    if r > 0:
        for p in range(length):
            j = local_of(scal_ref, y * length + p, length)
            add = o_ref[j + 4] * f_ref[2 * r - 2, p].astype(F32) + e_ref[j + 8] * f_ref[2 * r - 1, p].astype(F32)
            g_ref[p] = add if r == 1 else g_ref[p] + add
    advance(e_ref, 8, o_ref, 4, o_ref, 4, a_ref, c_ref, q_ref, wz_ref, wy_ref, 4, 2, 2 * r)


def side_steps(side, r, e_ref, o_ref, args, new):
    advance(e_ref, 8, o_ref, 4, o_ref, 4, *args, 12 if side == "a" else -4, 2, 2 * r)
    advance(o_ref, 4, e_ref, 8, e_ref, 8, *args, 8 if side == "a" else 0, 2, 2 * r + 1, extra=new)


def first_kernel(scal_ref, r_cur, r_lat, e_in, o_in, a_ref, c_ref, q_ref, wz_ref, wy_ref, e_ref, o_ref, new):
    length = r_cur.shape[0]
    y = scal_ref[2]
    for p in range(length):
        e_ref[halo_at(scal_ref, y, p, length, length) + 8] = r_cur[p]
    for p in range(length // 2):
        o_ref[halo_at(scal_ref, y, p, length // 2, length) + 4] = r_lat[p]
    side_steps("a", 0, e_ref, o_ref, (a_ref, c_ref, q_ref, wz_ref, wy_ref), new)


def side_kernel(scal_ref, *refs, r, side, recv, last):
    if recv:
        refs, recv_ref = refs[1:], refs[0]
    e_in, o_in, a_ref, c_ref, q_ref, wz_ref, wy_ref, e_ref, o_ref = refs[:9]
    new = None if last else refs[9]

    def work():
        if recv:
            for i in range(8):
                if side == "a":
                    e_ref[24 + i] = recv_ref[7 - i]
                else:
                    e_ref[7 - i] = recv_ref[i]
        side_steps(side, r, e_ref, o_ref, (a_ref, c_ref, q_ref, wz_ref, wy_ref), new)

    if last:
        own_a = (scal_ref[1] + scal_ref[2]) % 2
        pl.when(own_a == (1 if side == "a" else 0))(work)
    else:
        work()


def final_kernel(scal_ref, e_ref, o_ref, f_ref, g_in, field_ref, give_ref, keep_ref, *, steps):
    length, ny, _ = field_ref.shape
    y, core = scal_ref[2], scal_ref[3]
    part = ny // 4
    for p in range(length):
        j = local_of(scal_ref, y * length + p, length)
        last = e_ref[j + 8]
        field_ref[p] = last
        g = g_in[p] + o_ref[j + 4] * f_ref[steps - 2, p].astype(F32) + last * f_ref[steps - 1, p].astype(F32)
        for x in range(2):
            zero, one = g[2 * x * part : (2 * x + 1) * part], g[(2 * x + 1) * part : (2 * x + 2) * part]
            give_ref[p, x * part : (x + 1) * part] = jnp.where(core == 1, zero, one)
            keep_ref[p, x * part : (x + 1) * part] = jnp.where(core == 1, one, zero)


def pair_kernel(scal_ref, keep_ref, recv_ref, give_ref, mine_ref):
    x = scal_ref[4]
    part = give_ref.shape[1]
    for p in range(keep_ref.shape[0]):
        low = keep_ref[p, :part] + recv_ref[p, :part]
        high = keep_ref[p, part:] + recv_ref[p, part:]
        give_ref[p] = jnp.where(x == 1, low, high)
        mine_ref[p] = jnp.where(x == 1, high, low)


def call(kernel, out_shapes, args, aliases=None, free=(), flops=0, name=None):
    smem = pl.BlockSpec(memory_space=pltpu.SMEM)
    vm = pl.BlockSpec(memory_space=VM)
    specs = [smem if a.dtype == jnp.int32 and a.ndim == 1 else vm for a in args]
    args = [a if s is smem or i in free else vmem(a) for i, (a, s) in enumerate(zip(args, specs))]
    return pl.pallas_call(
        kernel,
        out_shape=out_shapes,
        in_specs=specs,
        out_specs=jax.tree.map(lambda _: vm, out_shapes),
        input_output_aliases=aliases or {},
        compiler_params=pltpu.CompilerParams(vmem_limit_bytes=LIMIT),
        cost_estimate=pl.CostEstimate(flops=flops, bytes_accessed=1 << 20, transcendentals=0),
        name=name,
    )(*args)


def shards(residual_traces, owners, surface_cells, trace_counts, start_current, start_later, forward_accel, courant_sq):
    traces = residual_traces[0]
    forward = forward_accel[0]
    cur, later = start_current[0], start_later[0]
    length, ny, nz = courant_sq.shape
    steps, width = traces.shape
    n, shots = lax.axis_size("space"), lax.axis_size("shot")
    levels = n // 2
    me, shot = lax.axis_index("space"), lax.axis_index("shot")
    level, y, core = me // 2, me % 2, shot % 2
    scal = jnp.stack([level, (level + core) % 2, y, core, shot // 2]).astype(jnp.int32)

    def move(x, pairs):
        return lax.ppermute(x, ("shot", "space"), pairs)

    def everywhere(space_pairs):
        return [(s * n + i, s * n + j) for s in range(shots) for i, j in space_pairs]

    def level_swap(parity):
        out = []
        for s in range(shots):
            for lv in range(levels - 1):
                if (lv + s) % 2 == parity:
                    for i in range(2):
                        lo = s * n + 2 * lv + i
                        out += [(lo, lo + 2), (lo + 2, lo)]
        return out

    swap_y = everywhere([(i, i ^ 1) for i in range(n)])
    down = [(2 * lv, 2 * lv - 2) for lv in range(1, levels)]
    up = [(2 * lv + 1, 2 * lv + 3) for lv in range(levels - 1)]
    direct = everywhere(down + up)
    relay = everywhere([(2 * lv, 2 * lv + 2) for lv in range(levels - 1)] + [(2 * lv + 1, 2 * lv - 1) for lv in range(1, levels)])
    swap_core = [(s * n + i, (s ^ 1) * n + i) for s in range(shots) for i in range(n)]
    swap_x = [(s * n + i, (s ^ 2) * n + i) for s in range(shots) for i in range(n)]
    swap_a, swap_b = level_swap(0), level_swap(1)

    half, two = length // 2, length // 4
    cut = lambda x, at, size: lax.dynamic_slice_in_dim(x, at, size, 0)
    y_cur = move(cur, swap_y)
    d_cur = move(cur, direct)
    c_edge = cut(courant_sq, half * y + two * core, two)
    c_rest = cut(courant_sq, half * (1 - y) + two * core, two)
    l_edge = cut(later, half * y, half)
    l_rest = cut(later, half * (1 - y), half)
    y_c = move(jnp.concatenate([c_edge, c_rest], 0), swap_y)
    d_edge = move(jnp.concatenate([l_edge, c_edge], 0), direct)
    y_edge = move(l_edge, swap_y)
    y_rest = move(l_rest, swap_y)

    number = me * width + jnp.arange(width, dtype=jnp.int32)
    live = jnp.where(number < trace_counts[0], 1.0, 0.0)
    code = (owners[0, :, 0] * (length * ny) + surface_cells[0]).astype(F32)
    gathered = jnp.concatenate([traces * live[None], code[None], jnp.zeros((16 - steps - 1, width), F32)], 0)[None]
    reach = 1
    while reach < n:
        gathered = jnp.concatenate([gathered, move(gathered, everywhere([(i, i ^ reach) for i in range(n)]))], 0)
        reach *= 2

    r_cur = move(y_cur, relay)
    r_c = move(y_c[:two], relay)
    r_lat = move(y_edge, relay)
    x_c = move(jnp.concatenate([y_c, d_edge[half:], r_c], 0), swap_core)

    plane = lambda k: VM((k, ny, nz), F32)
    e, o, wz, wy = call(
        field_kernel,
        [plane(32), plane(24), VM((2 * nz, nz), BF16), VM((4 * ny, 8 * ny), BF16)],
        [scal, cur, y_cur, later, y_edge, y_rest],
        free=(1, 3),
        name="fields",
    )
    q = call(
        functools.partial(q_kernel, steps=steps, length=length),
        VM((3, ny, 128), F32),
        [scal, gathered],
        name="receivers",
    )
    a, c, e, o = call(
        model_kernel,
        [plane(24), plane(24), plane(32), plane(24)],
        [scal, courant_sq, y_c, x_c, d_cur, d_edge, r_c, e, o],
        {7: 2, 8: 3},
        free=(1,),
        name="model",
    )
    g = jnp.zeros((length, ny, nz), F32)
    work = 2 * 16 * ny * nz * 60
    rounds = steps // 2
    send_a = send_b = None
    for r in range(rounds):
        if r:
            recv_a = move(send_a, swap_a)
            recv_b = move(send_b, swap_b)
        o, g = call(
            functools.partial(inner_kernel, r=r, length=length),
            [plane(24), plane(length)],
            [scal, e, o, a, c, q, wz, wy, forward, g],
            {2: 0, 9: 1},
            flops=work,
            name=f"inner{r}",
        )
        last = r == rounds - 1
        outs = [plane(32), plane(24)] + ([] if last else [plane(8)])
        model = [a, c, q, wz, wy]
        if r == 0:
            e, o, send_a = call(first_kernel, outs, [scal, r_cur, r_lat, e, o] + model, {3: 0, 4: 1}, flops=work, name="first")
            kern = functools.partial(side_kernel, r=r, side="b", recv=False, last=False)
            e, o, send_b = call(kern, outs, [scal, e, o] + model, {1: 0, 2: 1}, flops=work, name="side_b0")
            continue
        sent = []
        for side, recv in (("a", recv_a), ("b", recv_b)):
            kern = functools.partial(side_kernel, r=r, side=side, recv=True, last=last)
            e, o, *new = call(kern, outs, [scal, recv, e, o] + model, {2: 0, 3: 1}, flops=work, name=f"side_{side}{r}")
            sent += new
        if not last:
            send_a, send_b = sent

    part = ny // 4
    field, give, keep = call(
        functools.partial(final_kernel, steps=steps),
        [jax.ShapeDtypeStruct((length, ny, nz), F32), VM((length, 2 * part, nz), F32), VM((length, 2 * part, nz), F32)],
        [scal, e, o, forward, g],
        name="final",
    )
    give, mine = call(
        pair_kernel,
        [VM((length, part, nz), F32)] * 2,
        [scal, keep, move(give, swap_core)],
        name="pair",
    )
    return field[None], mine + move(give, swap_x)


def solution(mesh):
    placed = (
        P("shot", None, "space"),
        P("shot", "space", None),
        P("shot", "space"),
        P("shot"),
        P("shot", "space", None, None),
        P("shot", "space", None, None),
        P("shot", None, "space", None, None),
        P("space", None, None),
    )
    return jax.shard_map(
        shards,
        mesh=mesh,
        in_specs=placed,
        out_specs=(P("shot", "space", None, None), P("space", "shot", None)),
        check_vma=False,
    )
```

```python
import functools

import jax
import jax.numpy as jnp
from jax import lax
from jax.experimental import pallas as pl
from jax.experimental.pallas import tpu as pltpu
from jax.sharding import PartitionSpec as P

SCALE = 5040.0
TAPS = (8064.0, -1008.0, 128.0, -9.0)
CENTRE = 3.0 * (-205.0 / 72.0)

LIMIT = 16 * 1024 * 1024
VM = pltpu.VMEM
F32 = jnp.float32
BF16 = jnp.bfloat16


def vmem(x):
    return pltpu.with_memory_space_constraint(x, VM)


def band(rows, cols, block):
    r = lax.broadcasted_iota(jnp.int32, (rows, cols), 0)
    c = lax.broadcasted_iota(jnp.int32, (rows, cols), 1)
    r = r % cols
    c = c % rows
    gap = jnp.abs(r - c)
    out = jnp.zeros((rows, cols), F32)
    for j, w in enumerate(TAPS):
        out = jnp.where(gap == j + 1, w, out)
    return jnp.where(r // block == c // block, out, 0.0).astype(BF16)


def advance(src, so, prev, po, dst, do, a_ref, c_ref, q_ref, wz_ref, wy_ref, start, groups, k, extra=None):
    ny, nz = src.shape[1], src.shape[2]
    half = q_ref.shape[2]
    lane = lax.broadcasted_iota(jnp.int32, (ny, half), 1)
    for g in range(groups):
        t = start + 4 * g
        v = src[t + so : t + so + 4].reshape(4 * ny, nz)
        hi = v.astype(BF16)
        lo = (v - hi.astype(F32)).astype(BF16)
        s = jnp.dot(jnp.concatenate([hi, lo], 1), wz_ref[...], preferred_element_type=F32)
        s = s + jnp.dot(wy_ref[...], jnp.concatenate([hi, lo], 0), preferred_element_type=F32)
        for i in range(4):
            p = t + i
            total = s[i * ny : (i + 1) * ny]
            for j, w in enumerate(TAPS):
                total = total + w * (src[p + so + j + 1] + src[p + so - j - 1])
            fresh = a_ref[p + 4] * src[p + so] - prev[p + po] + c_ref[p + 4] * total
            x = p + 4
            shift = (2 - ((x % 8) * 16 + k)) % half
            q = q_ref[x // 8]
            q = jnp.where(lane == 2, pltpu.roll(q, shift, 1), 0.0)
            fresh = jnp.concatenate([fresh[:, :half] + q, fresh[:, half:]], 1)
            dst[p + do] = fresh
            if extra is not None:
                extra[p - start] = fresh


def local_of(scal_ref, g, length):
    return jnp.where(scal_ref[1] == 1, 2 * length - 1 - g, g)


def q_kernel(scal_ref, gathered_ref, q_ref, *, steps, length):
    n, rows, width = gathered_ref.shape
    across = q_ref.shape[1]
    level, odd = scal_ref[0], scal_ref[1]
    x_iota = lax.broadcasted_iota(jnp.int32, (8, 16, width), 0)
    y_iota = lax.broadcasted_iota(jnp.int32, (across, width), 0)

    def body(b, acc):
        block = gathered_ref[b]
        code = block[steps : steps + 1].astype(jnp.int32)
        gx = code // across
        y = code - gx * across
        gx = gx - level * (2 * length)
        x = jnp.where(odd == 1, 2 * length - 1 - gx, gx) + 4
        one_y = jnp.where(y_iota == y, 1.0, 0.0).astype(BF16)
        out = []
        for j in range(3):
            t = jnp.where(x_iota + 8 * j == x[None], block[None], 0.0).reshape(8 * 16, width)
            hi = t.astype(BF16)
            lo = (t - hi.astype(F32)).astype(BF16)
            dims = (((1,), (1,)), ((), ()))
            o = lax.dot_general(one_y, hi, dims, preferred_element_type=F32)
            o = o + lax.dot_general(one_y, lo, dims, preferred_element_type=F32)
            out.append(acc[j] + o)
        return tuple(out)

    zero = jnp.zeros(q_ref.shape[1:], F32)
    acc = lax.fori_loop(0, n, body, (zero, zero, zero))
    for j in range(3):
        q_ref[j] = acc[j]


def keep_if(flag, x):
    return jnp.where(flag == 1, x, 0.0)


def field_kernel(scal_ref, cur_own, cur_oth, lat_own, lat_edge, lat_rest, e_ref, o_ref, wz_ref, wy_ref):
    length, ny, nz = cur_own.shape
    half = length // 2
    y = scal_ref[2]
    for p in range(length):
        j = local_of(scal_ref, y * length + p, length)
        e_ref[j + 8] = cur_own[p]
        o_ref[j + 4] = lat_own[p]
        j = local_of(scal_ref, (1 - y) * length + p, length)
        e_ref[j + 8] = cur_oth[p]
    for p in range(half):
        j = local_of(scal_ref, (1 - y) * length + half * (1 - y) + p, length)
        o_ref[j + 4] = lat_edge[p]
        j = local_of(scal_ref, (1 - y) * length + half * y + p, length)
        o_ref[j + 4] = lat_rest[p]
    wz_ref[...] = band(2 * nz, nz, nz)
    wy_ref[...] = band(4 * ny, 8 * ny, ny)


def halo_at(scal_ref, upper, p, depth, length):
    g = jnp.where(upper == 1, 2 * length + p, p - depth)
    return local_of(scal_ref, g, length)


def model_kernel(scal_ref, c_own, c_oth, c_core, d_cur, d_edge, r_c, e_in, o_in, a_ref, c_ref, e_ref, o_ref):
    length = c_own.shape[0]
    half, two = length // 2, length // 4
    y, core = scal_ref[2], scal_ref[3]
    near, far = scal_ref[6 - y], scal_ref[5 + y]

    def put(j, cv):
        c_ref[j + 4] = cv * (1.0 / SCALE)
        a_ref[j + 4] = 2.0 + CENTRE * cv

    for p in range(length):
        put(local_of(scal_ref, y * length + p, length), c_own[p])
    base = (1 - y) * length
    for p in range(two):
        for who, piece, at in ((core, c_oth, 0), (1 - core, c_core, 0)):
            put(local_of(scal_ref, base + half * (1 - y) + two * who + p, length), piece[at + p])
            put(local_of(scal_ref, base + half * y + two * who + p, length), piece[at + two + p])
        put(halo_at(scal_ref, 1 - y, two * core + p, half, length), keep_if(near, d_edge[half + p]))
        put(halo_at(scal_ref, 1 - y, two * (1 - core) + p, half, length), keep_if(near, c_core[half + p]))
        put(halo_at(scal_ref, y, two * core + p, half, length), keep_if(far, r_c[p]))
        put(halo_at(scal_ref, y, two * (1 - core) + p, half, length), keep_if(far, c_core[half + two + p]))
    for p in range(length):
        e_ref[halo_at(scal_ref, 1 - y, p, length, length) + 8] = keep_if(near, d_cur[p])
    for p in range(half):
        o_ref[halo_at(scal_ref, 1 - y, p, half, length) + 4] = keep_if(near, d_edge[p])


def inner_kernel(scal_ref, e_ref, o_in, a_ref, c_ref, q_ref, wz_ref, wy_ref, f_ref, g_in, o_ref, g_ref, *, r, length):
    y = scal_ref[2]
    if r > 0:
        for p in range(length):
            j = local_of(scal_ref, y * length + p, length)
            add = o_ref[j + 4] * f_ref[2 * r - 2, p].astype(F32) + e_ref[j + 8] * f_ref[2 * r - 1, p].astype(F32)
            g_ref[p] = add if r == 1 else g_ref[p] + add
    advance(e_ref, 8, o_ref, 4, o_ref, 4, a_ref, c_ref, q_ref, wz_ref, wy_ref, 4, 2, 2 * r)


def side_steps(side, r, e_ref, o_ref, args, new):
    advance(e_ref, 8, o_ref, 4, o_ref, 4, *args, 12 if side == "a" else -4, 2, 2 * r)
    advance(o_ref, 4, e_ref, 8, e_ref, 8, *args, 8 if side == "a" else 0, 2, 2 * r + 1, extra=new)


def first_kernel(scal_ref, r_cur, r_lat, e_in, o_in, a_ref, c_ref, q_ref, wz_ref, wy_ref, e_ref, o_ref, new):
    length = r_cur.shape[0]
    y = scal_ref[2]
    far = scal_ref[5 + y]
    for p in range(length):
        e_ref[halo_at(scal_ref, y, p, length, length) + 8] = keep_if(far, r_cur[p])
    for p in range(length // 2):
        o_ref[halo_at(scal_ref, y, p, length // 2, length) + 4] = keep_if(far, r_lat[p])
    side_steps("a", 0, e_ref, o_ref, (a_ref, c_ref, q_ref, wz_ref, wy_ref), new)


def side_kernel(scal_ref, *refs, r, side, recv, last):
    if recv:
        refs, recv_ref = refs[1:], refs[0]
    e_in, o_in, a_ref, c_ref, q_ref, wz_ref, wy_ref, e_ref, o_ref = refs[:9]
    new = None if last else refs[9]

    def work():
        if recv:
            odd = scal_ref[1]
            inside = scal_ref[6 - odd] if side == "a" else scal_ref[5 + odd]
            for i in range(8):
                if side == "a":
                    e_ref[24 + i] = keep_if(inside, recv_ref[7 - i])
                else:
                    e_ref[7 - i] = keep_if(inside, recv_ref[i])
        side_steps(side, r, e_ref, o_ref, (a_ref, c_ref, q_ref, wz_ref, wy_ref), new)

    if last:
        own_a = (scal_ref[1] + scal_ref[2]) % 2
        pl.when(own_a == (1 if side == "a" else 0))(work)
    else:
        work()


def final_kernel(scal_ref, e_ref, o_ref, f_ref, g_in, field_ref, give_ref, keep_ref, *, steps):
    length, ny, _ = field_ref.shape
    y, core = scal_ref[2], scal_ref[3]
    part = ny // 4
    for p in range(length):
        j = local_of(scal_ref, y * length + p, length)
        last = e_ref[j + 8]
        field_ref[p] = last
        g = g_in[p] + o_ref[j + 4] * f_ref[steps - 2, p].astype(F32) + last * f_ref[steps - 1, p].astype(F32)
        for x in range(2):
            zero, one = g[2 * x * part : (2 * x + 1) * part], g[(2 * x + 1) * part : (2 * x + 2) * part]
            give_ref[p, x * part : (x + 1) * part] = jnp.where(core == 1, zero, one)
            keep_ref[p, x * part : (x + 1) * part] = jnp.where(core == 1, one, zero)


def pair_kernel(scal_ref, keep_ref, recv_ref, give_ref, mine_ref):
    x = scal_ref[4]
    part = give_ref.shape[1]
    for p in range(keep_ref.shape[0]):
        low = keep_ref[p, :part] + recv_ref[p, :part]
        high = keep_ref[p, part:] + recv_ref[p, part:]
        give_ref[p] = jnp.where(x == 1, low, high)
        mine_ref[p] = jnp.where(x == 1, high, low)


def call(kernel, out_shapes, args, aliases=None, free=(), flops=0, name=None):
    smem = pl.BlockSpec(memory_space=pltpu.SMEM)
    vm = pl.BlockSpec(memory_space=VM)
    specs = [smem if a.dtype == jnp.int32 and a.ndim == 1 else vm for a in args]
    args = [a if s is smem or i in free else vmem(a) for i, (a, s) in enumerate(zip(args, specs))]
    return pl.pallas_call(
        kernel,
        out_shape=out_shapes,
        in_specs=specs,
        out_specs=jax.tree.map(lambda _: vm, out_shapes),
        input_output_aliases=aliases or {},
        compiler_params=pltpu.CompilerParams(vmem_limit_bytes=LIMIT),
        cost_estimate=pl.CostEstimate(flops=flops, bytes_accessed=1 << 20, transcendentals=0),
        name=name,
    )(*args)


def shards(residual_traces, owners, surface_cells, trace_counts, start_current, start_later, forward_accel, courant_sq):
    traces = residual_traces[0]
    forward = forward_accel[0]
    cur, later = start_current[0], start_later[0]
    length, ny, nz = courant_sq.shape
    steps, width = traces.shape
    n, shots = lax.axis_size("space"), lax.axis_size("shot")
    levels = n // 2
    me, shot = lax.axis_index("space"), lax.axis_index("shot")
    level, y, core = me // 2, me % 2, shot % 2
    has_low = jnp.where(level > 0, 1, 0)
    has_high = jnp.where(level < levels - 1, 1, 0)
    scal = jnp.stack([level, level % 2, y, core, shot // 2, has_low, has_high]).astype(jnp.int32)

    def move(x, pairs):
        return lax.ppermute(x, ("shot", "space"), pairs)

    def everywhere(space_pairs):
        return [(s * n + i, s * n + j) for s in range(shots) for i, j in space_pairs]

    def level_swap(parity):
        out = []
        for s in range(shots):
            for lv in range(levels):
                up = lv % 2 == parity
                to = lv + 1 if up else lv - 1
                for i in range(2):
                    out.append((s * n + 2 * lv + i, s * n + (2 * to + i if 0 <= to < levels else 2 * lv + 1 - i)))
        return out

    swap_y = everywhere([(i, i ^ 1) for i in range(n)])
    hops = [(2 * lv, 2 * lv + 2) for lv in range(levels - 1)] + [(2 * lv + 1, 2 * lv - 1) for lv in range(1, levels)]
    relay = everywhere(hops)
    direct = [(j, i) for i, j in relay]
    swap_core = [(s * n + i, (s ^ 1) * n + i) for s in range(shots) for i in range(n)]
    swap_x = [(s * n + i, (s ^ 2) * n + i) for s in range(shots) for i in range(n)]
    swap_a, swap_b = level_swap(0), level_swap(1)

    def after(x, *others):
        return lax.optimization_barrier((x, *others))[0]

    half, two = length // 2, length // 4
    cut = lambda x, at, size: lax.dynamic_slice_in_dim(x, at, size, 0)
    y_cur = move(cur, swap_y)

    number = me * width + jnp.arange(width, dtype=jnp.int32)
    live = jnp.where(number < trace_counts[0], 1.0, 0.0)
    code = (owners[0, :, 0] * (length * ny) + surface_cells[0]).astype(F32)
    gathered = jnp.concatenate([traces * live[None], code[None], jnp.zeros((16 - steps - 1, width), F32)], 0)[None]
    reach = 1
    while reach < n:
        gathered = jnp.concatenate([gathered, move(gathered, everywhere([(i, i ^ reach) for i in range(n)]))], 0)
        if reach == 1:
            early = gathered
        reach *= 2

    c_edge = cut(courant_sq, half * y + two * core, two)
    c_rest = cut(courant_sq, half * (1 - y) + two * core, two)
    l_edge = cut(later, half * y, half)
    l_rest = cut(later, half * (1 - y), half)
    d_cur = move(cur, direct)
    y_c = move(after(jnp.concatenate([c_edge, c_rest], 0), early), swap_y)
    y_edge = move(after(l_edge, early), swap_y)
    y_rest = move(after(l_rest, early), swap_y)
    d_edge = move(after(jnp.concatenate([l_edge, c_edge], 0), gathered), direct)

    y_c = after(y_c, y_cur)
    y_edge = after(y_edge, y_c)
    y_rest = after(y_rest, y_edge)
    r_cur = move(y_cur, relay)
    r_c = move(y_c[:two], relay)
    r_lat = move(y_edge, relay)
    x_c = move(jnp.concatenate([y_c, d_edge[half:], r_c], 0), swap_core)

    plane = lambda k: VM((k, ny, nz), F32)
    e, o, wz, wy = call(
        field_kernel,
        [plane(32), plane(24), VM((2 * nz, nz), BF16), VM((4 * ny, 8 * ny), BF16)],
        [scal, cur, y_cur, later, y_edge, y_rest],
        free=(1, 3),
        name="fields",
    )
    q = call(
        functools.partial(q_kernel, steps=steps, length=length),
        VM((3, ny, 128), F32),
        [scal, gathered],
        name="receivers",
    )
    a, c, e, o = call(
        model_kernel,
        [plane(24), plane(24), plane(32), plane(24)],
        [scal, courant_sq, y_c, x_c, d_cur, d_edge, r_c, e, o],
        {7: 2, 8: 3},
        free=(1,),
        name="model",
    )
    g = jnp.zeros((length, ny, nz), F32)
    work = 2 * 16 * ny * nz * 60
    rounds = steps // 2
    send_a = send_b = None
    for r in range(rounds):
        if r:
            recv_a = move(send_a, swap_a)
            recv_b = move(send_b, swap_b)
        o, g = call(
            functools.partial(inner_kernel, r=r, length=length),
            [plane(24), plane(length)],
            [scal, e, o, a, c, q, wz, wy, forward, g],
            {2: 0, 9: 1},
            flops=work,
            name=f"inner{r}",
        )
        last = r == rounds - 1
        outs = [plane(32), plane(24)] + ([] if last else [plane(8)])
        model = [a, c, q, wz, wy]
        if r == 0:
            e, o, send_a = call(first_kernel, outs, [scal, r_cur, r_lat, e, o] + model, {3: 0, 4: 1}, flops=work, name="first")
            kern = functools.partial(side_kernel, r=r, side="b", recv=False, last=False)
            e, o, send_b = call(kern, outs, [scal, e, o] + model, {1: 0, 2: 1}, flops=work, name="side_b0")
            continue
        sent = []
        for side, recv in (("a", recv_a), ("b", recv_b)):
            kern = functools.partial(side_kernel, r=r, side=side, recv=True, last=last)
            e, o, *new = call(kern, outs, [scal, recv, e, o] + model, {2: 0, 3: 1}, flops=work, name=f"side_{side}{r}")
            sent += new
        if not last:
            send_a, send_b = sent

    part = ny // 4
    field, give, keep = call(
        functools.partial(final_kernel, steps=steps),
        [jax.ShapeDtypeStruct((length, ny, nz), F32), VM((length, 2 * part, nz), F32), VM((length, 2 * part, nz), F32)],
        [scal, e, o, forward, g],
        name="final",
    )
    give, mine = call(
        pair_kernel,
        [VM((length, part, nz), F32)] * 2,
        [scal, keep, move(give, swap_core)],
        name="pair",
    )
    return field[None], mine + move(give, swap_x)


def solution(mesh):
    placed = (
        P("shot", None, "space"),
        P("shot", "space", None),
        P("shot", "space"),
        P("shot"),
        P("shot", "space", None, None),
        P("shot", "space", None, None),
        P("shot", None, "space", None, None),
        P("space", None, None),
    )
    return jax.shard_map(
        shards,
        mesh=mesh,
        in_specs=placed,
        out_specs=(P("shot", "space", None, None), P("space", "shot", None)),
        check_vma=False,
    )
```

```python
import functools

import jax
import jax.numpy as jnp
from jax import lax
from jax.experimental import pallas as pl
from jax.experimental.pallas import tpu as pltpu
from jax.sharding import PartitionSpec as P

SCALE = 5040.0
TAPS = (8064.0, -1008.0, 128.0, -9.0)
CENTRE = 3.0 * (-205.0 / 72.0)

LIMIT = 16 * 1024 * 1024
VM = pltpu.VMEM
F32 = jnp.float32
BF16 = jnp.bfloat16


def vmem(x):
    return pltpu.with_memory_space_constraint(x, VM)


def band(rows, cols, block):
    r = lax.broadcasted_iota(jnp.int32, (rows, cols), 0)
    c = lax.broadcasted_iota(jnp.int32, (rows, cols), 1)
    r = r % cols
    c = c % rows
    gap = jnp.abs(r - c)
    out = jnp.zeros((rows, cols), F32)
    for j, w in enumerate(TAPS):
        out = jnp.where(gap == j + 1, w, out)
    return jnp.where(r // block == c // block, out, 0.0).astype(BF16)


def advance(src, so, prev, po, dst, do, a_ref, c_ref, q_ref, wz_ref, wy_ref, start, groups, k, extra=None):
    ny, nz = src.shape[1], src.shape[2]
    half = q_ref.shape[2]
    lane = lax.broadcasted_iota(jnp.int32, (ny, half), 1)
    for g in range(groups):
        t = start + 4 * g
        v = src[t + so : t + so + 4].reshape(4 * ny, nz)
        hi = v.astype(BF16)
        lo = (v - hi.astype(F32)).astype(BF16)
        s = jnp.dot(jnp.concatenate([hi, lo], 1), wz_ref[...], preferred_element_type=F32)
        s = s + jnp.dot(wy_ref[...], jnp.concatenate([hi, lo], 0), preferred_element_type=F32)
        for i in range(4):
            p = t + i
            total = s[i * ny : (i + 1) * ny]
            for j, w in enumerate(TAPS):
                total = total + w * (src[p + so + j + 1] + src[p + so - j - 1])
            fresh = a_ref[p + 4] * src[p + so] - prev[p + po] + c_ref[p + 4] * total
            x = p + 4
            shift = (2 - ((x % 8) * 16 + k)) % half
            q = q_ref[x // 8]
            q = jnp.where(lane == 2, pltpu.roll(q, shift, 1), 0.0)
            fresh = jnp.concatenate([fresh[:, :half] + q, fresh[:, half:]], 1)
            dst[p + do] = fresh
            if extra is not None:
                extra[p - start] = fresh


def local_of(scal_ref, g, length):
    return jnp.where(scal_ref[1] == 1, 2 * length - 1 - g, g)


def q_kernel(scal_ref, gathered_ref, q_ref, *, steps, length):
    n, rows, width = gathered_ref.shape
    across = q_ref.shape[1]
    level, odd = scal_ref[0], scal_ref[1]
    x_iota = lax.broadcasted_iota(jnp.int32, (8, 16, width), 0)
    y_iota = lax.broadcasted_iota(jnp.int32, (across, width), 0)

    def body(b, acc):
        block = gathered_ref[b]
        code = block[steps : steps + 1].astype(jnp.int32)
        gx = code // across
        y = code - gx * across
        gx = gx - level * (2 * length)
        x = jnp.where(odd == 1, 2 * length - 1 - gx, gx) + 4
        one_y = jnp.where(y_iota == y, 1.0, 0.0).astype(BF16)
        out = []
        for j in range(3):
            t = jnp.where(x_iota + 8 * j == x[None], block[None], 0.0).reshape(8 * 16, width)
            hi = t.astype(BF16)
            lo = (t - hi.astype(F32)).astype(BF16)
            dims = (((1,), (1,)), ((), ()))
            o = lax.dot_general(one_y, hi, dims, preferred_element_type=F32)
            o = o + lax.dot_general(one_y, lo, dims, preferred_element_type=F32)
            out.append(acc[j] + o)
        return tuple(out)

    zero = jnp.zeros(q_ref.shape[1:], F32)
    acc = lax.fori_loop(0, n, body, (zero, zero, zero))
    for j in range(3):
        q_ref[j] = acc[j]


def keep_if(flag, x):
    return jnp.where(flag == 1, x, 0.0)


def pack_kernel(scal_ref, later_ref, c_ref, edge_ref, rest_ref, sems):
    half = rest_ref.shape[0]
    two = half // 2
    y, core = scal_ref[2], scal_ref[3]
    copies = [
        (later_ref.at[pl.ds(half * y, half)], edge_ref.at[0:half]),
        (c_ref.at[pl.ds(half * y + two * core, two)], edge_ref.at[half : half + two]),
        (c_ref.at[pl.ds(half * (1 - y) + two * core, two)], edge_ref.at[half + two : 2 * half]),
        (later_ref.at[pl.ds(half * (1 - y), half)], rest_ref),
    ]
    copies = [pltpu.make_async_copy(src, dst, sems.at[i]) for i, (src, dst) in enumerate(copies)]
    for copy in copies:
        copy.start()
    for copy in copies:
        copy.wait()


def field_kernel(scal_ref, cur_own, cur_oth, lat_own, lat_edge, lat_rest, e_ref, o_ref, wz_ref, wy_ref):
    length, ny, nz = cur_own.shape
    half = length // 2
    y = scal_ref[2]
    for p in range(length):
        j = local_of(scal_ref, y * length + p, length)
        e_ref[j + 8] = cur_own[p]
        o_ref[j + 4] = lat_own[p]
        j = local_of(scal_ref, (1 - y) * length + p, length)
        e_ref[j + 8] = cur_oth[p]
    for p in range(half):
        j = local_of(scal_ref, (1 - y) * length + half * (1 - y) + p, length)
        o_ref[j + 4] = lat_edge[p]
        j = local_of(scal_ref, (1 - y) * length + half * y + p, length)
        o_ref[j + 4] = lat_rest[p]
    wz_ref[...] = band(2 * nz, nz, nz)
    wy_ref[...] = band(4 * ny, 8 * ny, ny)


def halo_at(scal_ref, upper, p, depth, length):
    g = jnp.where(upper == 1, 2 * length + p, p - depth)
    return local_of(scal_ref, g, length)


def model_kernel(scal_ref, c_own, m_oth, c_core, d_cur, d_edge, r_edge, e_in, o_in, a_ref, c_ref, e_ref, o_ref):
    length = c_own.shape[0]
    half, two = length // 2, length // 4
    y, core = scal_ref[2], scal_ref[3]
    near, far = scal_ref[6 - y], scal_ref[5 + y]

    def put(j, cv):
        c_ref[j + 4] = cv * (1.0 / SCALE)
        a_ref[j + 4] = 2.0 + CENTRE * cv

    for p in range(length):
        put(local_of(scal_ref, y * length + p, length), c_own[p])
    base = (1 - y) * length
    for p in range(two):
        for who, piece, at in ((core, m_oth, half), (1 - core, c_core, 0)):
            put(local_of(scal_ref, base + half * (1 - y) + two * who + p, length), piece[at + p])
            put(local_of(scal_ref, base + half * y + two * who + p, length), piece[at + two + p])
        put(halo_at(scal_ref, 1 - y, two * core + p, half, length), keep_if(near, d_edge[half + p]))
        put(halo_at(scal_ref, 1 - y, two * (1 - core) + p, half, length), keep_if(near, c_core[half + p]))
        put(halo_at(scal_ref, y, two * core + p, half, length), keep_if(far, r_edge[half + p]))
        put(halo_at(scal_ref, y, two * (1 - core) + p, half, length), keep_if(far, c_core[half + two + p]))
    for p in range(length):
        e_ref[halo_at(scal_ref, 1 - y, p, length, length) + 8] = keep_if(near, d_cur[p])
    for p in range(half):
        o_ref[halo_at(scal_ref, 1 - y, p, half, length) + 4] = keep_if(near, d_edge[p])
        o_ref[halo_at(scal_ref, y, p, half, length) + 4] = keep_if(far, r_edge[p])


def inner_kernel(scal_ref, e_ref, o_in, a_ref, c_ref, q_ref, wz_ref, wy_ref, f_ref, g_in, o_ref, g_ref, *, r, length):
    y = scal_ref[2]
    if r > 0:
        for p in range(length):
            j = local_of(scal_ref, y * length + p, length)
            add = o_ref[j + 4] * f_ref[2 * r - 2, p].astype(F32) + e_ref[j + 8] * f_ref[2 * r - 1, p].astype(F32)
            g_ref[p] = add if r == 1 else g_ref[p] + add
    advance(e_ref, 8, o_ref, 4, o_ref, 4, a_ref, c_ref, q_ref, wz_ref, wy_ref, 4, 2, 2 * r)


def side_steps(side, r, e_ref, o_ref, args, new):
    advance(e_ref, 8, o_ref, 4, o_ref, 4, *args, 12 if side == "a" else -4, 2, 2 * r)
    advance(o_ref, 4, e_ref, 8, e_ref, 8, *args, 8 if side == "a" else 0, 2, 2 * r + 1, extra=new)


def first_kernel(scal_ref, r_cur, e_in, o_in, a_ref, c_ref, q_ref, wz_ref, wy_ref, e_ref, o_ref, new):
    length = r_cur.shape[0]
    y = scal_ref[2]
    far = scal_ref[5 + y]
    for p in range(length):
        e_ref[halo_at(scal_ref, y, p, length, length) + 8] = keep_if(far, r_cur[p])
    side_steps("a", 0, e_ref, o_ref, (a_ref, c_ref, q_ref, wz_ref, wy_ref), new)


def side_kernel(scal_ref, *refs, r, side, recv, last):
    if recv:
        refs, recv_ref = refs[1:], refs[0]
    e_in, o_in, a_ref, c_ref, q_ref, wz_ref, wy_ref, e_ref, o_ref = refs[:9]
    new = None if last else refs[9]

    def work():
        if recv:
            odd = scal_ref[1]
            inside = scal_ref[6 - odd] if side == "a" else scal_ref[5 + odd]
            for i in range(8):
                if side == "a":
                    e_ref[24 + i] = keep_if(inside, recv_ref[7 - i])
                else:
                    e_ref[7 - i] = keep_if(inside, recv_ref[i])
        side_steps(side, r, e_ref, o_ref, (a_ref, c_ref, q_ref, wz_ref, wy_ref), new)

    if last:
        own_a = (scal_ref[1] + scal_ref[2]) % 2
        pl.when(own_a == (1 if side == "a" else 0))(work)
    else:
        work()


def final_kernel(scal_ref, e_ref, o_ref, f_ref, g_in, field_ref, give_ref, keep_ref, *, steps):
    length, ny, _ = field_ref.shape
    y, core = scal_ref[2], scal_ref[3]
    part = ny // 4
    for p in range(length):
        j = local_of(scal_ref, y * length + p, length)
        last = e_ref[j + 8]
        field_ref[p] = last
        g = g_in[p] + o_ref[j + 4] * f_ref[steps - 2, p].astype(F32) + last * f_ref[steps - 1, p].astype(F32)
        for x in range(2):
            zero, one = g[2 * x * part : (2 * x + 1) * part], g[(2 * x + 1) * part : (2 * x + 2) * part]
            give_ref[p, x * part : (x + 1) * part] = jnp.where(core == 1, zero, one)
            keep_ref[p, x * part : (x + 1) * part] = jnp.where(core == 1, one, zero)


def pair_kernel(scal_ref, keep_ref, recv_ref, give_ref, mine_ref):
    x = scal_ref[4]
    part = give_ref.shape[1]
    for p in range(keep_ref.shape[0]):
        low = keep_ref[p, :part] + recv_ref[p, :part]
        high = keep_ref[p, part:] + recv_ref[p, part:]
        give_ref[p] = jnp.where(x == 1, low, high)
        mine_ref[p] = jnp.where(x == 1, high, low)


def call(kernel, out_shapes, args, aliases=None, free=(), flops=0, name=None):
    smem = pl.BlockSpec(memory_space=pltpu.SMEM)
    vm = pl.BlockSpec(memory_space=VM)
    specs = [smem if a.dtype == jnp.int32 and a.ndim == 1 else vm for a in args]
    args = [a if s is smem or i in free else vmem(a) for i, (a, s) in enumerate(zip(args, specs))]
    return pl.pallas_call(
        kernel,
        out_shape=out_shapes,
        in_specs=specs,
        out_specs=jax.tree.map(lambda _: vm, out_shapes),
        input_output_aliases=aliases or {},
        compiler_params=pltpu.CompilerParams(vmem_limit_bytes=LIMIT),
        cost_estimate=pl.CostEstimate(flops=flops, bytes_accessed=1 << 20, transcendentals=0),
        name=name,
    )(*args)


def shards(residual_traces, owners, surface_cells, trace_counts, start_current, start_later, forward_accel, courant_sq):
    traces = residual_traces[0]
    forward = forward_accel[0]
    cur, later = start_current[0], start_later[0]
    length, ny, nz = courant_sq.shape
    steps, width = traces.shape
    n, shots = lax.axis_size("space"), lax.axis_size("shot")
    levels = n // 2
    me, shot = lax.axis_index("space"), lax.axis_index("shot")
    level, y, core = me // 2, me % 2, shot % 2
    has_low = jnp.where(level > 0, 1, 0)
    has_high = jnp.where(level < levels - 1, 1, 0)
    scal = jnp.stack([level, level % 2, y, core, shot // 2, has_low, has_high]).astype(jnp.int32)

    def move(x, pairs):
        return lax.ppermute(x, ("shot", "space"), pairs)

    def everywhere(space_pairs):
        return [(s * n + i, s * n + j) for s in range(shots) for i, j in space_pairs]

    def level_swap(parity):
        out = []
        for s in range(shots):
            for lv in range(levels):
                up = lv % 2 == parity
                to = lv + 1 if up else lv - 1
                for i in range(2):
                    out.append((s * n + 2 * lv + i, s * n + (2 * to + i if 0 <= to < levels else 2 * lv + 1 - i)))
        return out

    swap_y = everywhere([(i, i ^ 1) for i in range(n)])
    hops = [(2 * lv, 2 * lv + 2) for lv in range(levels - 1)] + [(2 * lv + 1, 2 * lv - 1) for lv in range(1, levels)]
    relay = everywhere(hops)
    direct = [(j, i) for i, j in relay]
    swap_core = [(s * n + i, (s ^ 1) * n + i) for s in range(shots) for i in range(n)]
    swap_x = [(s * n + i, (s ^ 2) * n + i) for s in range(shots) for i in range(n)]
    swap_a, swap_b = level_swap(0), level_swap(1)

    def after(x, *others):
        return lax.optimization_barrier((x, *others))[0]

    number = me * width + jnp.arange(width, dtype=jnp.int32)
    live = jnp.where(number < trace_counts[0], 1.0, 0.0)
    code = (owners[0, :, 0] * (length * ny) + surface_cells[0]).astype(F32)
    gathered = jnp.concatenate([traces * live[None], code[None], jnp.zeros((16 - steps - 1, width), F32)], 0)[None]
    reach = 2
    while reach < n:
        gathered = jnp.concatenate([gathered, move(gathered, everywhere([(i, i ^ reach) for i in range(n)]))], 0)
        reach *= 2

    half, two = length // 2, length // 4
    plane = lambda k: VM((k, ny, nz), F32)
    edge, rest = pl.pallas_call(
        pack_kernel,
        out_shape=[plane(length), plane(half)],
        in_specs=[pl.BlockSpec(memory_space=pltpu.SMEM)] + [pl.BlockSpec(memory_space=pl.ANY)] * 2,
        out_specs=[pl.BlockSpec(memory_space=VM)] * 2,
        scratch_shapes=[pltpu.SemaphoreType.DMA((4,))],
        compiler_params=pltpu.CompilerParams(vmem_limit_bytes=LIMIT),
        name="pack",
    )(scal, *[pltpu.with_memory_space_constraint(x, pltpu.HBM) for x in (later, courant_sq)])
    y_edge = move(edge, swap_y)
    y_cur = move(after(cur, edge), swap_y)
    y_rest = move(after(rest, y_edge), swap_y)
    d_edge = move(after(edge, gathered), direct)
    d_cur = move(after(cur, gathered), direct)
    gathered = jnp.concatenate([gathered, move(gathered, swap_y)], 0)
    r_edge = move(y_edge, relay)
    r_cur = move(after(y_cur, gathered), relay)
    x_c = move(jnp.concatenate([y_edge[half:], d_edge[half : half + two], r_edge[half : half + two]], 0), swap_core)

    e, o, wz, wy = call(
        field_kernel,
        [plane(32), plane(24), VM((2 * nz, nz), BF16), VM((4 * ny, 8 * ny), BF16)],
        [scal, cur, y_cur, later, y_edge, y_rest],
        free=(1, 3),
        name="fields",
    )
    q = call(
        functools.partial(q_kernel, steps=steps, length=length),
        VM((3, ny, 128), F32),
        [scal, gathered],
        name="receivers",
    )
    a, c, e, o = call(
        model_kernel,
        [plane(24), plane(24), plane(32), plane(24)],
        [scal, courant_sq, y_edge, x_c, d_cur, d_edge, r_edge, e, o],
        {7: 2, 8: 3},
        free=(1,),
        name="model",
    )
    g = jnp.zeros((length, ny, nz), F32)
    work = 2 * 16 * ny * nz * 60
    rounds = steps // 2
    send_a = send_b = None
    for r in range(rounds):
        if r:
            recv_a = move(send_a, swap_a)
            recv_b = move(send_b, swap_b)
        o, g = call(
            functools.partial(inner_kernel, r=r, length=length),
            [plane(24), plane(length)],
            [scal, e, o, a, c, q, wz, wy, forward, g],
            {2: 0, 9: 1},
            flops=work,
            name=f"inner{r}",
        )
        last = r == rounds - 1
        outs = [plane(32), plane(24)] + ([] if last else [plane(8)])
        model = [a, c, q, wz, wy]
        if r == 0:
            e, o, send_a = call(first_kernel, outs, [scal, r_cur, e, o] + model, {2: 0, 3: 1}, flops=work, name="first")
            kern = functools.partial(side_kernel, r=r, side="b", recv=False, last=False)
            e, o, send_b = call(kern, outs, [scal, e, o] + model, {1: 0, 2: 1}, flops=work, name="side_b0")
            continue
        sent = []
        for side, recv in (("a", recv_a), ("b", recv_b)):
            kern = functools.partial(side_kernel, r=r, side=side, recv=True, last=last)
            e, o, *new = call(kern, outs, [scal, recv, e, o] + model, {2: 0, 3: 1}, flops=work, name=f"side_{side}{r}")
            sent += new
        if not last:
            send_a, send_b = sent

    part = ny // 4
    field, give, keep = call(
        functools.partial(final_kernel, steps=steps),
        [jax.ShapeDtypeStruct((length, ny, nz), F32), VM((length, 2 * part, nz), F32), VM((length, 2 * part, nz), F32)],
        [scal, e, o, forward, g],
        name="final",
    )
    give, mine = call(
        pair_kernel,
        [VM((length, part, nz), F32)] * 2,
        [scal, keep, move(give, swap_core)],
        name="pair",
    )
    return field[None], mine + move(give, swap_x)


def solution(mesh):
    placed = (
        P("shot", None, "space"),
        P("shot", "space", None),
        P("shot", "space"),
        P("shot"),
        P("shot", "space", None, None),
        P("shot", "space", None, None),
        P("shot", None, "space", None, None),
        P("space", None, None),
    )
    return jax.shard_map(
        shards,
        mesh=mesh,
        in_specs=placed,
        out_specs=(P("shot", "space", None, None), P("space", "shot", None)),
        check_vma=False,
    )
```

```python
import functools

import jax
import jax.numpy as jnp
from jax import lax
from jax.experimental import pallas as pl
from jax.experimental.pallas import tpu as pltpu
from jax.sharding import PartitionSpec as P

SCALE = 5040.0
TAPS = (8064.0, -1008.0, 128.0, -9.0)
CENTRE = 3.0 * (-205.0 / 72.0)

LIMIT = 16 * 1024 * 1024
VM = pltpu.VMEM
F32 = jnp.float32
BF16 = jnp.bfloat16


def vmem(x):
    return pltpu.with_memory_space_constraint(x, VM)


def band(rows, cols, block):
    r = lax.broadcasted_iota(jnp.int32, (rows, cols), 0)
    c = lax.broadcasted_iota(jnp.int32, (rows, cols), 1)
    r = r % cols
    c = c % rows
    gap = jnp.abs(r - c)
    out = jnp.zeros((rows, cols), F32)
    for j, w in enumerate(TAPS):
        out = jnp.where(gap == j + 1, w, out)
    return jnp.where(r // block == c // block, out, 0.0).astype(BF16)


def advance(src, so, prev, po, dst, do, a_ref, c_ref, q_ref, wz_ref, wy_ref, start, groups, k, extra=None):
    ny, nz = src.shape[1], src.shape[2]
    half = q_ref.shape[2]
    lane = lax.broadcasted_iota(jnp.int32, (ny, half), 1)
    for g in range(groups):
        t = start + 4 * g
        v = src[t + so : t + so + 4].reshape(4 * ny, nz)
        hi = v.astype(BF16)
        lo = (v - hi.astype(F32)).astype(BF16)
        s = jnp.dot(jnp.concatenate([hi, lo], 1), wz_ref[...], preferred_element_type=F32)
        s = s + jnp.dot(wy_ref[...], jnp.concatenate([hi, lo], 0), preferred_element_type=F32)
        for i in range(4):
            p = t + i
            total = s[i * ny : (i + 1) * ny]
            for j, w in enumerate(TAPS):
                total = total + w * (src[p + so + j + 1] + src[p + so - j - 1])
            fresh = a_ref[p + 4] * src[p + so] - prev[p + po] + c_ref[p + 4] * total
            x = p + 4
            shift = (2 - ((x % 8) * 16 + k)) % half
            q = q_ref[x // 8]
            q = jnp.where(lane == 2, pltpu.roll(q, shift, 1), 0.0)
            fresh = jnp.concatenate([fresh[:, :half] + q, fresh[:, half:]], 1)
            dst[p + do] = fresh
            if extra is not None:
                extra[p - start] = fresh


def local_of(scal_ref, g, length):
    return jnp.where(scal_ref[1] == 1, 2 * length - 1 - g, g)


def q_kernel(scal_ref, gathered_ref, q_ref, *, steps, length):
    n, rows, width = gathered_ref.shape
    across = q_ref.shape[1]
    level, odd = scal_ref[0], scal_ref[1]
    x_iota = lax.broadcasted_iota(jnp.int32, (8, 16, width), 0)
    y_iota = lax.broadcasted_iota(jnp.int32, (across, width), 0)

    def body(b, acc):
        block = gathered_ref[b]
        code = block[steps : steps + 1].astype(jnp.int32)
        gx = code // across
        y = code - gx * across
        gx = gx - level * (2 * length)
        x = jnp.where(odd == 1, 2 * length - 1 - gx, gx) + 4
        one_y = jnp.where(y_iota == y, 1.0, 0.0).astype(BF16)
        out = []
        for j in range(3):
            t = jnp.where(x_iota + 8 * j == x[None], block[None], 0.0).reshape(8 * 16, width)
            hi = t.astype(BF16)
            lo = (t - hi.astype(F32)).astype(BF16)
            dims = (((1,), (1,)), ((), ()))
            o = lax.dot_general(one_y, hi, dims, preferred_element_type=F32)
            o = o + lax.dot_general(one_y, lo, dims, preferred_element_type=F32)
            out.append(acc[j] + o)
        return tuple(out)

    zero = jnp.zeros(q_ref.shape[1:], F32)
    acc = lax.fori_loop(0, n, body, (zero, zero, zero))
    for j in range(3):
        q_ref[j] = acc[j]


def keep_if(flag, x):
    return jnp.where(flag == 1, x, 0.0)


def pack_kernel(scal_ref, later_ref, c_ref, edge_ref, rest_ref, sems):
    half = edge_ref.shape[0] // 2
    y = scal_ref[2]
    copies = []
    for out, at in ((edge_ref, half * y), (rest_ref, half * (1 - y))):
        for i, src in enumerate((later_ref, c_ref)):
            copies.append((src.at[pl.ds(at, half)], out.at[i * half : (i + 1) * half]))
    copies = [pltpu.make_async_copy(src, dst, sems.at[i]) for i, (src, dst) in enumerate(copies)]
    for copy in copies:
        copy.start()
    for copy in copies:
        copy.wait()


def cur_kernel(scal_ref, own, other, e_ref, send_a, send_b):
    length = own.shape[0]
    y = scal_ref[2]
    for p in range(length):
        e_ref[local_of(scal_ref, y * length + p, length) + 8] = own[p]
        e_ref[local_of(scal_ref, (1 - y) * length + p, length) + 8] = other[p]
    send_a[...] = e_ref[16:24]
    send_b[...] = e_ref[8:16]


def edge_kernel(scal_ref, own, other, send_a, send_b):
    half = own.shape[0] // 2
    odd = scal_ref[1]

    def put(dst, src):
        for p in range(half):
            at = jnp.where(odd == 1, half - 1 - p, p)
            dst[at] = src[p]
            dst[half + at] = src[half + p]

    def split(a, b):
        put(send_a, a)
        put(send_b, b)

    own_a = (odd + scal_ref[2]) % 2
    pl.when(own_a == 1)(lambda: split(own, other))
    pl.when(own_a == 0)(lambda: split(other, own))


def model_kernel(scal_ref, c_own, lat_own, edge, rest, o_ref, a_ref, c_ref, wz_ref, wy_ref):
    length, ny, nz = c_own.shape
    half = length // 2
    y = scal_ref[2]

    def put(g, later, cv):
        j = local_of(scal_ref, g, length) + 4
        o_ref[j] = later
        c_ref[j] = cv * (1.0 / SCALE)
        a_ref[j] = 2.0 + CENTRE * cv

    for p in range(length):
        put(y * length + p, lat_own[p], c_own[p])
    base = (1 - y) * length
    for p in range(half):
        put(base + half * (1 - y) + p, edge[p], edge[half + p])
        put(base + half * y + p, rest[p], rest[half + p])
    wz_ref[...] = band(2 * nz, nz, nz)
    wy_ref[...] = band(4 * ny, 8 * ny, ny)


def inner_kernel(scal_ref, e_ref, o_in, a_ref, c_ref, q_ref, wz_ref, wy_ref, f_ref, g_in, o_ref, g_ref, *, r, length):
    y = scal_ref[2]
    if r > 0:
        for p in range(length):
            j = local_of(scal_ref, y * length + p, length)
            add = o_ref[j + 4] * f_ref[2 * r - 2, p].astype(F32) + e_ref[j + 8] * f_ref[2 * r - 1, p].astype(F32)
            g_ref[p] = add if r == 1 else g_ref[p] + add
    advance(e_ref, 8, o_ref, 4, o_ref, 4, a_ref, c_ref, q_ref, wz_ref, wy_ref, 4, 2, 2 * r)


def side_steps(side, r, e_ref, o_ref, args, new):
    advance(e_ref, 8, o_ref, 4, o_ref, 4, *args, 12 if side == "a" else -4, 2, 2 * r)
    advance(o_ref, 4, e_ref, 8, e_ref, 8, *args, 8 if side == "a" else 0, 2, 2 * r + 1, extra=new)


def side_kernel(scal_ref, recv_ref, *refs, r, side, last):
    if r == 0:
        edge_ref, e_in, o_in, a_in, c_in, q_ref, wz_ref, wy_ref, e_ref, o_ref, a_ref, c_ref, new = refs
    else:
        e_in, o_in, a_ref, c_ref, q_ref, wz_ref, wy_ref, e_ref, o_ref = refs[:9]
        new = None if last else refs[9]

    def work():
        odd = scal_ref[1]
        inside = scal_ref[6 - odd] if side == "a" else scal_ref[5 + odd]
        for i in range(8):
            if side == "a":
                e_ref[24 + i] = keep_if(inside, recv_ref[7 - i])
            else:
                e_ref[7 - i] = keep_if(inside, recv_ref[i])
        if r == 0:
            for i in range(4):
                to, at = (20 + i, 3 - i) if side == "a" else (3 - i, i)
                o_ref[to] = keep_if(inside, edge_ref[at])
                cv = keep_if(inside, edge_ref[4 + at])
                c_ref[to] = cv * (1.0 / SCALE)
                a_ref[to] = 2.0 + CENTRE * cv
        side_steps(side, r, e_ref, o_ref, (a_ref, c_ref, q_ref, wz_ref, wy_ref), new)

    if last:
        own_a = (scal_ref[1] + scal_ref[2]) % 2
        pl.when(own_a == (1 if side == "a" else 0))(work)
    else:
        work()


def final_kernel(scal_ref, e_ref, o_ref, f_ref, g_in, field_ref, give_ref, keep_ref, *, steps):
    length, ny, _ = field_ref.shape
    y, core = scal_ref[2], scal_ref[3]
    part = ny // 4
    for p in range(length):
        j = local_of(scal_ref, y * length + p, length)
        last = e_ref[j + 8]
        field_ref[p] = last
        g = g_in[p] + o_ref[j + 4] * f_ref[steps - 2, p].astype(F32) + last * f_ref[steps - 1, p].astype(F32)
        for x in range(2):
            zero, one = g[2 * x * part : (2 * x + 1) * part], g[(2 * x + 1) * part : (2 * x + 2) * part]
            give_ref[p, x * part : (x + 1) * part] = jnp.where(core == 1, zero, one)
            keep_ref[p, x * part : (x + 1) * part] = jnp.where(core == 1, one, zero)


def pair_kernel(scal_ref, keep_ref, recv_ref, give_ref, mine_ref):
    x = scal_ref[4]
    part = give_ref.shape[1]
    for p in range(keep_ref.shape[0]):
        low = keep_ref[p, :part] + recv_ref[p, :part]
        high = keep_ref[p, part:] + recv_ref[p, part:]
        give_ref[p] = jnp.where(x == 1, low, high)
        mine_ref[p] = jnp.where(x == 1, high, low)


def call(kernel, out_shapes, args, aliases=None, free=(), flops=0, name=None):
    smem = pl.BlockSpec(memory_space=pltpu.SMEM)
    vm = pl.BlockSpec(memory_space=VM)
    specs = [smem if a.dtype == jnp.int32 and a.ndim == 1 else vm for a in args]
    args = [a if s is smem or i in free else vmem(a) for i, (a, s) in enumerate(zip(args, specs))]
    return pl.pallas_call(
        kernel,
        out_shape=out_shapes,
        in_specs=specs,
        out_specs=jax.tree.map(lambda _: vm, out_shapes),
        input_output_aliases=aliases or {},
        compiler_params=pltpu.CompilerParams(vmem_limit_bytes=LIMIT),
        cost_estimate=pl.CostEstimate(flops=flops, bytes_accessed=1 << 20, transcendentals=0),
        name=name,
    )(*args)


def shards(residual_traces, owners, surface_cells, trace_counts, start_current, start_later, forward_accel, courant_sq):
    traces = residual_traces[0]
    forward = forward_accel[0]
    cur, later = start_current[0], start_later[0]
    length, ny, nz = courant_sq.shape
    steps, width = traces.shape
    n, shots = lax.axis_size("space"), lax.axis_size("shot")
    levels = n // 2
    me, shot = lax.axis_index("space"), lax.axis_index("shot")
    level, y, core = me // 2, me % 2, shot % 2
    has_low = jnp.where(level > 0, 1, 0)
    has_high = jnp.where(level < levels - 1, 1, 0)
    scal = jnp.stack([level, level % 2, y, core, shot // 2, has_low, has_high]).astype(jnp.int32)

    def move(x, pairs):
        return lax.ppermute(x, ("shot", "space"), pairs)

    def everywhere(space_pairs):
        return [(s * n + i, s * n + j) for s in range(shots) for i, j in space_pairs]

    def level_swap(parity):
        out = []
        for s in range(shots):
            for lv in range(levels):
                up = lv % 2 == parity
                to = lv + 1 if up else lv - 1
                for i in range(2):
                    out.append((s * n + 2 * lv + i, s * n + (2 * to + i if 0 <= to < levels else 2 * lv + 1 - i)))
        return out

    swap_y = everywhere([(i, i ^ 1) for i in range(n)])
    swap_core = [(s * n + i, (s ^ 1) * n + i) for s in range(shots) for i in range(n)]
    swap_x = [(s * n + i, (s ^ 2) * n + i) for s in range(shots) for i in range(n)]
    swap_a, swap_b = level_swap(0), level_swap(1)
    near_a, near_b = [[(i, j) for i, j in p if i ^ j != 1] for p in (swap_a, swap_b)]

    def after(x, *others):
        return lax.optimization_barrier((x, *others))[0]

    number = me * width + jnp.arange(width, dtype=jnp.int32)
    live = jnp.where(number < trace_counts[0], 1.0, 0.0)
    code = (owners[0, :, 0] * (length * ny) + surface_cells[0]).astype(F32)
    gathered = jnp.concatenate([traces * live[None], code[None], jnp.zeros((16 - steps - 1, width), F32)], 0)[None]
    reach = 2
    while reach < n:
        gathered = jnp.concatenate([gathered, move(gathered, everywhere([(i, i ^ reach) for i in range(n)]))], 0)
        if reach == 2:
            early = gathered
        reach *= 2

    half = length // 2
    plane = lambda k: VM((k, ny, nz), F32)
    edge, rest = pl.pallas_call(
        pack_kernel,
        out_shape=[plane(length), plane(length)],
        in_specs=[pl.BlockSpec(memory_space=pltpu.SMEM)] + [pl.BlockSpec(memory_space=pl.ANY)] * 2,
        out_specs=[pl.BlockSpec(memory_space=VM)] * 2,
        scratch_shapes=[pltpu.SemaphoreType.DMA((4,))],
        compiler_params=pltpu.CompilerParams(vmem_limit_bytes=LIMIT),
        name="pack",
    )(scal, *[pltpu.with_memory_space_constraint(x, pltpu.HBM) for x in (later, courant_sq)])
    y_cur = move(cur, swap_y)
    y_edge = move(after(edge, early), swap_y)
    y_rest = move(after(rest, early), swap_y)

    e, send_a, send_b = call(cur_kernel, [plane(32), plane(8), plane(8)], [scal, cur, y_cur], free=(1,), name="field")
    recv_a, recv_b = move(send_a, near_a), move(send_b, near_b)
    gathered = jnp.concatenate([gathered, move(after(gathered, recv_b), swap_y)], 0)
    edge_a, edge_b = call(edge_kernel, [plane(8), plane(8)], [scal, edge, y_edge], name="edges")
    edge_a, edge_b = move(edge_a, near_a), move(edge_b, near_b)
    q = call(
        functools.partial(q_kernel, steps=steps, length=length),
        VM((3, ny, 128), F32),
        [scal, gathered],
        name="receivers",
    )
    o, a, c, wz, wy = call(
        model_kernel,
        [plane(24), plane(24), plane(24), VM((2 * nz, nz), BF16), VM((4 * ny, 8 * ny), BF16)],
        [scal, courant_sq, later, y_edge, y_rest],
        free=(1, 2),
        name="model",
    )
    g = jnp.zeros((length, ny, nz), F32)
    work = 2 * 16 * ny * nz * 60
    rounds = steps // 2
    for r in range(rounds):
        if r:
            recv_a = move(send_a, swap_a)
            recv_b = move(send_b, swap_b)
        o, g = call(
            functools.partial(inner_kernel, r=r, length=length),
            [plane(24), plane(length)],
            [scal, e, o, a, c, q, wz, wy, forward, g],
            {2: 0, 9: 1},
            flops=work,
            name=f"inner{r}",
        )
        last = r == rounds - 1
        sent = []
        for side in "ab":
            got = [recv_a if side == "a" else recv_b]
            if r == 0:
                got.append(edge_a if side == "a" else edge_b)
            kept = 4 if r == 0 else 2
            at = 1 + len(got)
            e, o, *new = call(
                functools.partial(side_kernel, r=r, side=side, last=last),
                [plane(32), plane(24), plane(24), plane(24)][:kept] + ([] if last else [plane(8)]),
                [scal, *got, e, o, a, c, q, wz, wy],
                {at + i: i for i in range(kept)},
                flops=work,
                name=f"side_{side}{r}",
            )
            if r == 0:
                a, c, *new = new
            sent += new
        if not last:
            send_a, send_b = sent

    part = ny // 4
    field, give, keep = call(
        functools.partial(final_kernel, steps=steps),
        [jax.ShapeDtypeStruct((length, ny, nz), F32), VM((length, 2 * part, nz), F32), VM((length, 2 * part, nz), F32)],
        [scal, e, o, forward, g],
        name="final",
    )
    give, mine = call(
        pair_kernel,
        [VM((length, part, nz), F32)] * 2,
        [scal, keep, move(give, swap_core)],
        name="pair",
    )
    return field[None], mine + move(give, swap_x)


def solution(mesh):
    placed = (
        P("shot", None, "space"),
        P("shot", "space", None),
        P("shot", "space"),
        P("shot"),
        P("shot", "space", None, None),
        P("shot", "space", None, None),
        P("shot", None, "space", None, None),
        P("space", None, None),
    )
    return jax.shard_map(
        shards,
        mesh=mesh,
        in_specs=placed,
        out_specs=(P("shot", "space", None, None), P("space", "shot", None)),
        check_vma=False,
    )
```

```python
import functools

import jax
import jax.numpy as jnp
from jax import lax
from jax.experimental import pallas as pl
from jax.experimental.pallas import tpu as pltpu
from jax.sharding import PartitionSpec as P

SCALE = 5040.0
TAPS = (8064.0, -1008.0, 128.0, -9.0)
CENTRE = 3.0 * (-205.0 / 72.0)

LIMIT = 16 * 1024 * 1024
VM = pltpu.VMEM
F32 = jnp.float32
BF16 = jnp.bfloat16


def vmem(x):
    return pltpu.with_memory_space_constraint(x, VM)


def band(rows, cols, block):
    r = lax.broadcasted_iota(jnp.int32, (rows, cols), 0)
    c = lax.broadcasted_iota(jnp.int32, (rows, cols), 1)
    r = r % cols
    c = c % rows
    gap = jnp.abs(r - c)
    out = jnp.zeros((rows, cols), F32)
    for j, w in enumerate(TAPS):
        out = jnp.where(gap == j + 1, w, out)
    return jnp.where(r // block == c // block, out, 0.0).astype(BF16)


def advance(src, so, prev, po, dst, do, a_ref, c_ref, q_ref, wz_ref, wy_ref, start, groups, k, extra=None):
    ny, nz = src.shape[1], src.shape[2]
    half = q_ref.shape[2]
    lane = lax.broadcasted_iota(jnp.int32, (ny, half), 1)
    for g in range(groups):
        t = start + 4 * g
        v = src[t + so : t + so + 4].reshape(4 * ny, nz)
        hi = v.astype(BF16)
        lo = (v - hi.astype(F32)).astype(BF16)
        s = jnp.dot(jnp.concatenate([hi, lo], 1), wz_ref[...], preferred_element_type=F32)
        s = s + jnp.dot(wy_ref[...], jnp.concatenate([hi, lo], 0), preferred_element_type=F32)
        for i in range(4):
            p = t + i
            total = s[i * ny : (i + 1) * ny]
            for j, w in enumerate(TAPS):
                total = total + w * (src[p + so + j + 1] + src[p + so - j - 1])
            fresh = a_ref[p + 4] * src[p + so] - prev[p + po] + c_ref[p + 4] * total
            x = p + 4
            shift = (2 - ((x % 8) * 16 + k)) % half
            q = q_ref[x // 8]
            q = jnp.where(lane == 2, pltpu.roll(q, shift, 1), 0.0)
            fresh = jnp.concatenate([fresh[:, :half] + q, fresh[:, half:]], 1)
            dst[p + do] = fresh
            if extra is not None:
                extra[p - start] = fresh


def local_of(scal_ref, g, length):
    return jnp.where(scal_ref[1] == 1, 2 * length - 1 - g, g)


def q_kernel(scal_ref, gathered_ref, q_ref, *, steps, length):
    n, rows, width = gathered_ref.shape
    across = q_ref.shape[1]
    level, odd = scal_ref[0], scal_ref[1]
    x_iota = lax.broadcasted_iota(jnp.int32, (8, 16, width), 0)
    y_iota = lax.broadcasted_iota(jnp.int32, (across, width), 0)

    def body(b, acc):
        block = gathered_ref[b]
        code = block[steps : steps + 1].astype(jnp.int32)
        gx = code // across
        y = code - gx * across
        gx = gx - level * (2 * length)
        x = jnp.where(odd == 1, 2 * length - 1 - gx, gx) + 4
        one_y = jnp.where(y_iota == y, 1.0, 0.0).astype(BF16)
        out = []
        for j in range(3):
            t = jnp.where(x_iota + 8 * j == x[None], block[None], 0.0).reshape(8 * 16, width)
            hi = t.astype(BF16)
            lo = (t - hi.astype(F32)).astype(BF16)
            dims = (((1,), (1,)), ((), ()))
            o = lax.dot_general(one_y, hi, dims, preferred_element_type=F32)
            o = o + lax.dot_general(one_y, lo, dims, preferred_element_type=F32)
            out.append(acc[j] + o)
        return tuple(out)

    zero = jnp.zeros(q_ref.shape[1:], F32)
    acc = lax.fori_loop(0, n, body, (zero, zero, zero))
    for j in range(3):
        q_ref[j] = acc[j]


def keep_if(flag, x):
    return jnp.where(flag == 1, x, 0.0)


def pack_kernel(scal_ref, later_ref, c_ref, edge_ref, rest_ref, sems):
    half = edge_ref.shape[0] // 2
    y = scal_ref[2]
    copies = []
    for out, at in ((edge_ref, half * y), (rest_ref, half * (1 - y))):
        for i, src in enumerate((later_ref, c_ref)):
            copies.append((src.at[pl.ds(at, half)], out.at[i * half : (i + 1) * half]))
    copies = [pltpu.make_async_copy(src, dst, sems.at[i]) for i, (src, dst) in enumerate(copies)]
    for copy in copies:
        copy.start()
    for copy in copies:
        copy.wait()


def cur_kernel(scal_ref, own, other, e_ref, send_a, send_b):
    length = own.shape[0]
    y = scal_ref[2]
    for p in range(length):
        e_ref[local_of(scal_ref, y * length + p, length) + 8] = own[p]
        e_ref[local_of(scal_ref, (1 - y) * length + p, length) + 8] = other[p]
    send_a[...] = e_ref[16:24]
    send_b[...] = e_ref[8:16]


def edge_kernel(scal_ref, own, other, send_a, send_b):
    half = own.shape[0] // 2
    odd = scal_ref[1]

    def put(dst, src):
        for p in range(half):
            at = jnp.where(odd == 1, half - 1 - p, p)
            dst[at] = src[p]
            dst[half + at] = src[half + p]

    def split(a, b):
        put(send_a, a)
        put(send_b, b)

    own_a = (odd + scal_ref[2]) % 2
    pl.when(own_a == 1)(lambda: split(own, other))
    pl.when(own_a == 0)(lambda: split(other, own))


def model_kernel(scal_ref, c_own, lat_own, edge, rest, o_ref, a_ref, c_ref, wz_ref, wy_ref):
    length, ny, nz = c_own.shape
    half = length // 2
    y = scal_ref[2]

    def put(g, later, cv):
        j = local_of(scal_ref, g, length) + 4
        o_ref[j] = later
        c_ref[j] = cv * (1.0 / SCALE)
        a_ref[j] = 2.0 + CENTRE * cv

    for p in range(length):
        put(y * length + p, lat_own[p], c_own[p])
    base = (1 - y) * length
    for p in range(half):
        put(base + half * (1 - y) + p, edge[p], edge[half + p])
        put(base + half * y + p, rest[p], rest[half + p])
    wz_ref[...] = band(2 * nz, nz, nz)
    wy_ref[...] = band(4 * ny, 8 * ny, ny)


def inner_kernel(scal_ref, e_ref, o_in, a_ref, c_ref, q_ref, wz_ref, wy_ref, f_ref, g_in, o_ref, g_ref, *, r, length):
    y = scal_ref[2]
    if r > 0:
        for p in range(length):
            j = local_of(scal_ref, y * length + p, length)
            add = o_ref[j + 4] * f_ref[2 * r - 2, p].astype(F32) + e_ref[j + 8] * f_ref[2 * r - 1, p].astype(F32)
            g_ref[p] = add if r == 1 else g_ref[p] + add
    advance(e_ref, 8, o_ref, 4, o_ref, 4, a_ref, c_ref, q_ref, wz_ref, wy_ref, 4, 2, 2 * r)


def side_steps(side, r, e_ref, o_ref, args, new):
    advance(e_ref, 8, o_ref, 4, o_ref, 4, *args, 12 if side == "a" else -4, 2, 2 * r)
    advance(o_ref, 4, e_ref, 8, e_ref, 8, *args, 8 if side == "a" else 0, 2, 2 * r + 1, extra=new)


def side_kernel(scal_ref, recv_ref, *refs, r, side, last):
    if r == 0:
        edge_ref, e_in, o_in, a_in, c_in, q_ref, wz_ref, wy_ref, e_ref, o_ref, a_ref, c_ref, new = refs
    else:
        e_in, o_in, a_ref, c_ref, q_ref, wz_ref, wy_ref, e_ref, o_ref = refs[:9]
        new = None if last else refs[9]

    def work():
        odd = scal_ref[1]
        inside = scal_ref[6 - odd] if side == "a" else scal_ref[5 + odd]
        for i in range(8):
            if side == "a":
                e_ref[24 + i] = keep_if(inside, recv_ref[7 - i])
            else:
                e_ref[7 - i] = keep_if(inside, recv_ref[i])
        if r == 0:
            for i in range(4):
                to, at = (20 + i, 3 - i) if side == "a" else (3 - i, i)
                o_ref[to] = keep_if(inside, edge_ref[at])
                cv = keep_if(inside, edge_ref[4 + at])
                c_ref[to] = cv * (1.0 / SCALE)
                a_ref[to] = 2.0 + CENTRE * cv
        side_steps(side, r, e_ref, o_ref, (a_ref, c_ref, q_ref, wz_ref, wy_ref), new)

    if last:
        own_a = (scal_ref[1] + scal_ref[2]) % 2
        pl.when(own_a == (1 if side == "a" else 0))(work)
    else:
        work()


def share_kernel(scal_ref, e_ref, o_ref, f_ref, g_in, g_ref, *, steps, give):
    length, rows, _ = g_ref.shape
    part = rows // 2
    y, core = scal_ref[2], scal_ref[3]
    mine = 1 - core if give else core
    for p in range(length):
        j = local_of(scal_ref, y * length + p, length)
        for x in range(2):
            at = pl.ds(pl.multiple_of(part * (2 * x + mine), part), part)
            g_ref[p, x * part : (x + 1) * part] = (
                g_in[p, at]
                + o_ref[j + 4, at] * f_ref[steps - 2, p, at].astype(F32)
                + e_ref[j + 8, at] * f_ref[steps - 1, p, at].astype(F32)
            )


def pair_kernel(scal_ref, keep_ref, recv_ref, give_ref):
    x = scal_ref[4]
    part = give_ref.shape[1]
    at = pl.ds(pl.multiple_of(part * (1 - x), part), part)
    for p in range(keep_ref.shape[0]):
        give_ref[p] = keep_ref[p, at] + recv_ref[p, at]


def own_kernel(scal_ref, e_ref, keep_ref, recv_ref, late_ref, field_ref, mine_ref):
    x = scal_ref[4]
    length, part, _ = mine_ref.shape
    at = pl.ds(pl.multiple_of(part * x, part), part)
    for p in range(length):
        field_ref[p] = e_ref[local_of(scal_ref, scal_ref[2] * length + p, length) + 8]
        mine_ref[p] = keep_ref[p, at] + recv_ref[p, at]


def call(kernel, out_shapes, args, aliases=None, free=(), flops=0, name=None):
    smem = pl.BlockSpec(memory_space=pltpu.SMEM)
    vm = pl.BlockSpec(memory_space=VM)
    specs = [smem if a.dtype == jnp.int32 and a.ndim == 1 else vm for a in args]
    args = [a if s is smem or i in free else vmem(a) for i, (a, s) in enumerate(zip(args, specs))]
    return pl.pallas_call(
        kernel,
        out_shape=out_shapes,
        in_specs=specs,
        out_specs=jax.tree.map(lambda _: vm, out_shapes),
        input_output_aliases=aliases or {},
        compiler_params=pltpu.CompilerParams(vmem_limit_bytes=LIMIT),
        cost_estimate=pl.CostEstimate(flops=flops, bytes_accessed=1 << 20, transcendentals=0),
        name=name,
    )(*args)


def shards(residual_traces, owners, surface_cells, trace_counts, start_current, start_later, forward_accel, courant_sq):
    traces = residual_traces[0]
    forward = forward_accel[0]
    cur, later = start_current[0], start_later[0]
    length, ny, nz = courant_sq.shape
    steps, width = traces.shape
    n, shots = lax.axis_size("space"), lax.axis_size("shot")
    levels = n // 2
    me, shot = lax.axis_index("space"), lax.axis_index("shot")
    level, y, core = me // 2, me % 2, shot % 2
    has_low = jnp.where(level > 0, 1, 0)
    has_high = jnp.where(level < levels - 1, 1, 0)
    scal = jnp.stack([level, level % 2, y, core, shot // 2, has_low, has_high]).astype(jnp.int32)

    def move(x, pairs):
        return lax.ppermute(x, ("shot", "space"), pairs)

    def everywhere(space_pairs):
        return [(s * n + i, s * n + j) for s in range(shots) for i, j in space_pairs]

    def level_swap(parity):
        out = []
        for s in range(shots):
            for lv in range(levels):
                up = lv % 2 == parity
                to = lv + 1 if up else lv - 1
                for i in range(2):
                    at = 2 * lv + i
                    out.append((s * n + at, s * n + 2 * to + i if 0 <= to < levels else (s ^ 1) * n + at))
        return out

    swap_y = everywhere([(i, i ^ 1) for i in range(n)])
    swap_core = [(s * n + i, (s ^ 1) * n + i) for s in range(shots) for i in range(n)]
    swap_x = [(s * n + i, (s ^ 2) * n + i) for s in range(shots) for i in range(n)]
    swap_a, swap_b = level_swap(0), level_swap(1)
    near_a, near_b = [[(i, j) for i, j in p if i // n == j // n] for p in (swap_a, swap_b)]

    def after(x, *others):
        return lax.optimization_barrier((x, *others))[0]

    number = me * width + jnp.arange(width, dtype=jnp.int32)
    live = jnp.where(number < trace_counts[0], 1.0, 0.0)
    code = (owners[0, :, 0] * (length * ny) + surface_cells[0]).astype(F32)
    gathered = jnp.concatenate([traces * live[None], code[None], jnp.zeros((16 - steps - 1, width), F32)], 0)[None]
    reach = 2
    while reach < n:
        gathered = jnp.concatenate([gathered, move(gathered, everywhere([(i, i ^ reach) for i in range(n)]))], 0)
        if reach == 2:
            early = gathered
        reach *= 2

    half = length // 2
    plane = lambda k: VM((k, ny, nz), F32)
    edge, rest = pl.pallas_call(
        pack_kernel,
        out_shape=[plane(length), plane(length)],
        in_specs=[pl.BlockSpec(memory_space=pltpu.SMEM)] + [pl.BlockSpec(memory_space=pl.ANY)] * 2,
        out_specs=[pl.BlockSpec(memory_space=VM)] * 2,
        scratch_shapes=[pltpu.SemaphoreType.DMA((4,))],
        compiler_params=pltpu.CompilerParams(vmem_limit_bytes=LIMIT),
        name="pack",
    )(scal, *[pltpu.with_memory_space_constraint(x, pltpu.HBM) for x in (later, courant_sq)])
    y_cur = move(cur, swap_y)
    y_edge = move(after(edge, early), swap_y)
    y_rest = move(after(rest, early), swap_y)

    e, send_a, send_b = call(cur_kernel, [plane(32), plane(8), plane(8)], [scal, cur, after(y_cur, gathered)], free=(1,), name="field")
    recv_a, recv_b = move(send_a, near_a), move(send_b, near_b)
    gathered = jnp.concatenate([gathered, move(after(gathered, recv_b), swap_y)], 0)
    edge_a, edge_b = call(edge_kernel, [plane(8), plane(8)], [scal, edge, y_edge], name="edges")
    edge_a, edge_b = move(edge_a, near_a), move(edge_b, near_b)
    q = call(
        functools.partial(q_kernel, steps=steps, length=length),
        VM((3, ny, 128), F32),
        [scal, gathered],
        name="receivers",
    )
    o, a, c, wz, wy = call(
        model_kernel,
        [plane(24), plane(24), plane(24), VM((2 * nz, nz), BF16), VM((4 * ny, 8 * ny), BF16)],
        [scal, courant_sq, later, y_edge, y_rest],
        free=(1, 2),
        name="model",
    )
    g = jnp.zeros((length, ny, nz), F32)
    work = 2 * 16 * ny * nz * 60
    rounds = steps // 2
    for r in range(rounds):
        if r:
            recv_a = move(send_a, swap_a)
            recv_b = move(send_b, swap_b)
        o, g = call(
            functools.partial(inner_kernel, r=r, length=length),
            [plane(24), plane(length)],
            [scal, e, o, a, c, q, wz, wy, forward, g],
            {2: 0, 9: 1},
            flops=work,
            name=f"inner{r}",
        )
        last = r == rounds - 1
        sent = []
        for side in "ab":
            got = [recv_a if side == "a" else recv_b]
            if r == 0:
                got.append(edge_a if side == "a" else edge_b)
            kept = 4 if r == 0 else 2
            at = 1 + len(got)
            e, o, *new = call(
                functools.partial(side_kernel, r=r, side=side, last=last),
                [plane(32), plane(24), plane(24), plane(24)][:kept] + ([] if last else [plane(8)]),
                [scal, *got, e, o, a, c, q, wz, wy],
                {at + i: i for i in range(kept)},
                flops=work,
                name=f"side_{side}{r}",
            )
            if r == 0:
                a, c, *new = new
            sent += new
        if not last:
            send_a, send_b = sent

    part = ny // 4
    shares = [scal, e, o, forward, g]
    share = VM((length, 2 * part, nz), F32)
    give = call(functools.partial(share_kernel, steps=steps, give=True), [share], shares, name="give")[0]
    recv = move(give, swap_core)
    keep = call(functools.partial(share_kernel, steps=steps, give=False), [share], shares, name="keep")[0]
    give = call(pair_kernel, [VM((length, part, nz), F32)], [scal, keep, recv], name="pair")[0]
    last = move(give, swap_x)
    field, mine = call(
        own_kernel,
        [jax.ShapeDtypeStruct((length, ny, nz), F32), VM((length, part, nz), F32)],
        [scal, e, keep, recv, give],
        flops=work,
        name="own",
    )
    return field[None], mine + last


def solution(mesh):
    placed = (
        P("shot", None, "space"),
        P("shot", "space", None),
        P("shot", "space"),
        P("shot"),
        P("shot", "space", None, None),
        P("shot", "space", None, None),
        P("shot", None, "space", None, None),
        P("space", None, None),
    )
    return jax.shard_map(
        shards,
        mesh=mesh,
        in_specs=placed,
        out_specs=(P("shot", "space", None, None), P("space", "shot", None)),
        check_vma=False,
    )
```

```python
import functools

import jax
import jax.numpy as jnp
from jax import lax
from jax.experimental import pallas as pl
from jax.experimental.pallas import tpu as pltpu
from jax.sharding import PartitionSpec as P

SCALE = 5040.0
TAPS = (8064.0, -1008.0, 128.0, -9.0)
CENTRE = 3.0 * (-205.0 / 72.0)

LIMIT = 16 * 1024 * 1024
VM = pltpu.VMEM
F32 = jnp.float32
BF16 = jnp.bfloat16


def vmem(x):
    return pltpu.with_memory_space_constraint(x, VM)


def band(rows, cols, block):
    r = lax.broadcasted_iota(jnp.int32, (rows, cols), 0)
    c = lax.broadcasted_iota(jnp.int32, (rows, cols), 1)
    r = r % cols
    c = c % rows
    gap = jnp.abs(r - c)
    out = jnp.zeros((rows, cols), F32)
    for j, w in enumerate(TAPS):
        out = jnp.where(gap == j + 1, w, out)
    return jnp.where(r // block == c // block, out, 0.0).astype(BF16)


def advance(src, so, prev, po, dst, do, a_ref, c_ref, q_ref, wz_ref, wy_ref, start, groups, k, extra=None):
    ny, nz = src.shape[1], src.shape[2]
    half = q_ref.shape[2]
    lane = lax.broadcasted_iota(jnp.int32, (ny, half), 1)
    for g in range(groups):
        t = start + 4 * g
        v = src[t + so : t + so + 4].reshape(4 * ny, nz)
        hi = v.astype(BF16)
        lo = (v - hi.astype(F32)).astype(BF16)
        s = jnp.dot(jnp.concatenate([hi, lo], 1), wz_ref[...], preferred_element_type=F32)
        s = s + jnp.dot(wy_ref[...], jnp.concatenate([hi, lo], 0), preferred_element_type=F32)
        for i in range(4):
            p = t + i
            total = s[i * ny : (i + 1) * ny]
            for j, w in enumerate(TAPS):
                total = total + w * (src[p + so + j + 1] + src[p + so - j - 1])
            fresh = a_ref[p + 4] * src[p + so] - prev[p + po] + c_ref[p + 4] * total
            x = p + 4
            shift = (2 - ((x % 8) * 16 + k)) % half
            q = q_ref[x // 8]
            q = jnp.where(lane == 2, pltpu.roll(q, shift, 1), 0.0)
            fresh = jnp.concatenate([fresh[:, :half] + q, fresh[:, half:]], 1)
            dst[p + do] = fresh
            if extra is not None:
                extra[p - start] = fresh


def local_of(scal_ref, g, length):
    return jnp.where(scal_ref[1] == 1, 2 * length - 1 - g, g)


def q_kernel(scal_ref, gathered_ref, q_ref, *, steps, length):
    n, rows, width = gathered_ref.shape
    across = q_ref.shape[1]
    level, odd = scal_ref[0], scal_ref[1]
    x_iota = lax.broadcasted_iota(jnp.int32, (8, 16, width), 0)
    y_iota = lax.broadcasted_iota(jnp.int32, (across, width), 0)

    def body(b, acc):
        block = gathered_ref[b]
        code = block[steps : steps + 1].astype(jnp.int32)
        gx = code // across
        y = code - gx * across
        gx = gx - level * (2 * length)
        x = jnp.where(odd == 1, 2 * length - 1 - gx, gx) + 4
        one_y = jnp.where(y_iota == y, 1.0, 0.0).astype(BF16)
        out = []
        for j in range(3):
            t = jnp.where(x_iota + 8 * j == x[None], block[None], 0.0).reshape(8 * 16, width)
            hi = t.astype(BF16)
            lo = (t - hi.astype(F32)).astype(BF16)
            dims = (((1,), (1,)), ((), ()))
            o = lax.dot_general(one_y, hi, dims, preferred_element_type=F32)
            o = o + lax.dot_general(one_y, lo, dims, preferred_element_type=F32)
            out.append(acc[j] + o)
        return tuple(out)

    zero = jnp.zeros(q_ref.shape[1:], F32)
    acc = lax.fori_loop(0, n, body, (zero, zero, zero), unroll=4)
    for j in range(3):
        q_ref[j] = acc[j]


def keep_if(flag, x):
    return jnp.where(flag == 1, x, 0.0)


def pack_kernel(scal_ref, later_ref, c_ref, edge_ref, rest_ref, sems):
    half = edge_ref.shape[0] // 2
    y = scal_ref[2]
    copies = []
    for out, at in ((edge_ref, half * y), (rest_ref, half * (1 - y))):
        for i, src in enumerate((later_ref, c_ref)):
            copies.append((src.at[pl.ds(at, half)], out.at[i * half : (i + 1) * half]))
    copies = [pltpu.make_async_copy(src, dst, sems.at[i]) for i, (src, dst) in enumerate(copies)]
    for copy in copies:
        copy.start()
    for copy in copies:
        copy.wait()


def cur_kernel(scal_ref, own, other, e_ref, send_a, send_b):
    length = own.shape[0]
    y = scal_ref[2]
    for p in range(length):
        e_ref[local_of(scal_ref, y * length + p, length) + 8] = own[p]
        e_ref[local_of(scal_ref, (1 - y) * length + p, length) + 8] = other[p]
    send_a[...] = e_ref[16:24]
    send_b[...] = e_ref[8:16]


def edge_kernel(scal_ref, own, other, send_a, send_b):
    half = own.shape[0] // 2
    odd = scal_ref[1]

    def put(dst, src):
        for p in range(half):
            at = jnp.where(odd == 1, half - 1 - p, p)
            dst[at] = src[p]
            dst[half + at] = src[half + p]

    def split(a, b):
        put(send_a, a)
        put(send_b, b)

    own_a = (odd + scal_ref[2]) % 2
    pl.when(own_a == 1)(lambda: split(own, other))
    pl.when(own_a == 0)(lambda: split(other, own))


def model_kernel(scal_ref, c_own, lat_own, edge, rest, o_ref, a_ref, c_ref, wz_ref, wy_ref):
    length, ny, nz = c_own.shape
    half = length // 2
    y = scal_ref[2]

    def put(g, later, cv):
        j = local_of(scal_ref, g, length) + 4
        o_ref[j] = later
        c_ref[j] = cv * (1.0 / SCALE)
        a_ref[j] = 2.0 + CENTRE * cv

    for p in range(length):
        put(y * length + p, lat_own[p], c_own[p])
    base = (1 - y) * length
    for p in range(half):
        put(base + half * (1 - y) + p, edge[p], edge[half + p])
        put(base + half * y + p, rest[p], rest[half + p])
    wz_ref[...] = band(2 * nz, nz, nz)
    wy_ref[...] = band(4 * ny, 8 * ny, ny)


def start_kernel(scal_ref, recv_a, recv_b, e_in, o_in, a_ref, c_ref, q_ref, wz_ref, wy_ref, e_ref, o_ref):
    odd = scal_ref[1]
    for i in range(8):
        e_ref[24 + i] = keep_if(scal_ref[6 - odd], recv_a[7 - i])
        e_ref[7 - i] = keep_if(scal_ref[5 + odd], recv_b[i])
    advance(e_ref, 8, o_ref, 4, o_ref, 4, a_ref, c_ref, q_ref, wz_ref, wy_ref, 0, 4, 0)


def inner_kernel(scal_ref, e_ref, o_in, a_ref, c_ref, q_ref, wz_ref, wy_ref, f_ref, g_in, o_ref, g_ref, *, r, length):
    y = scal_ref[2]
    if r > 0:
        for p in range(length):
            j = local_of(scal_ref, y * length + p, length)
            add = o_ref[j + 4] * f_ref[2 * r - 2, p].astype(F32) + e_ref[j + 8] * f_ref[2 * r - 1, p].astype(F32)
            g_ref[p] = add if r == 1 else g_ref[p] + add
    advance(e_ref, 8, o_ref, 4, o_ref, 4, a_ref, c_ref, q_ref, wz_ref, wy_ref, 4, 2, 2 * r)


def side_kernel(scal_ref, recv_ref, e_in, o_in, a_in, c_in, q_ref, wz_ref, wy_ref, e_ref, o_ref, *outs, r, side, last):
    if r == 0:
        a_ref, c_ref, new = outs
    else:
        a_ref, c_ref, new = a_in, c_in, None if last else outs[0]

    def work():
        odd = scal_ref[1]
        inside = scal_ref[6 - odd] if side == "a" else scal_ref[5 + odd]
        args = (a_ref, c_ref, q_ref, wz_ref, wy_ref)
        if r == 0:
            for i in range(4):
                to, at = (20 + i, 3 - i) if side == "a" else (3 - i, i)
                o_ref[to] = keep_if(inside, recv_ref[at])
                cv = keep_if(inside, recv_ref[4 + at])
                c_ref[to] = cv * (1.0 / SCALE)
                a_ref[to] = 2.0 + CENTRE * cv
            advance(e_ref, 8, o_ref, 4, o_ref, 4, *args, 16 if side == "a" else -4, 1, 0)
        else:
            for i in range(8):
                if side == "a":
                    e_ref[24 + i] = keep_if(inside, recv_ref[7 - i])
                else:
                    e_ref[7 - i] = keep_if(inside, recv_ref[i])
            advance(e_ref, 8, o_ref, 4, o_ref, 4, *args, 12 if side == "a" else -4, 2, 2 * r)
        advance(o_ref, 4, e_ref, 8, e_ref, 8, *args, 8 if side == "a" else 0, 2, 2 * r + 1, extra=new)

    if last:
        own_a = (scal_ref[1] + scal_ref[2]) % 2
        pl.when(own_a == (1 if side == "a" else 0))(work)
    else:
        work()


def share_kernel(scal_ref, e_ref, o_ref, f_ref, g_in, g_ref, *, steps, give):
    length, rows, _ = g_ref.shape
    part = rows // 2
    y, core = scal_ref[2], scal_ref[3]
    mine = 1 - core if give else core
    for p in range(length):
        j = local_of(scal_ref, y * length + p, length)
        for x in range(2):
            at = pl.ds(pl.multiple_of(part * (2 * x + mine), part), part)
            g_ref[p, x * part : (x + 1) * part] = (
                g_in[p, at]
                + o_ref[j + 4, at] * f_ref[steps - 2, p, at].astype(F32)
                + e_ref[j + 8, at] * f_ref[steps - 1, p, at].astype(F32)
            )


def pair_kernel(scal_ref, keep_ref, recv_ref, give_ref):
    x = scal_ref[4]
    part = give_ref.shape[1]
    at = pl.ds(pl.multiple_of(part * (1 - x), part), part)
    for p in range(keep_ref.shape[0]):
        give_ref[p] = keep_ref[p, at] + recv_ref[p, at]


def own_kernel(scal_ref, e_ref, keep_ref, recv_ref, late_ref, field_ref, mine_ref):
    x = scal_ref[4]
    length, part, _ = mine_ref.shape
    at = pl.ds(pl.multiple_of(part * x, part), part)
    for p in range(length):
        field_ref[p] = e_ref[local_of(scal_ref, scal_ref[2] * length + p, length) + 8]
        mine_ref[p] = keep_ref[p, at] + recv_ref[p, at]


def call(kernel, out_shapes, args, aliases=None, free=(), flops=0, name=None):
    smem = pl.BlockSpec(memory_space=pltpu.SMEM)
    vm = pl.BlockSpec(memory_space=VM)
    specs = [smem if a.dtype == jnp.int32 and a.ndim == 1 else vm for a in args]
    args = [a if s is smem or i in free else vmem(a) for i, (a, s) in enumerate(zip(args, specs))]
    return pl.pallas_call(
        kernel,
        out_shape=out_shapes,
        in_specs=specs,
        out_specs=jax.tree.map(lambda _: vm, out_shapes),
        input_output_aliases=aliases or {},
        compiler_params=pltpu.CompilerParams(vmem_limit_bytes=LIMIT),
        cost_estimate=pl.CostEstimate(flops=flops, bytes_accessed=1 << 20, transcendentals=0),
        name=name,
    )(*args)


def shards(residual_traces, owners, surface_cells, trace_counts, start_current, start_later, forward_accel, courant_sq):
    traces = residual_traces[0]
    forward = forward_accel[0]
    cur, later = start_current[0], start_later[0]
    length, ny, nz = courant_sq.shape
    steps, width = traces.shape
    n, shots = lax.axis_size("space"), lax.axis_size("shot")
    levels = n // 2
    me, shot = lax.axis_index("space"), lax.axis_index("shot")
    level, y, core = me // 2, me % 2, shot % 2
    has_low = jnp.where(level > 0, 1, 0)
    has_high = jnp.where(level < levels - 1, 1, 0)
    scal = jnp.stack([level, level % 2, y, core, shot // 2, has_low, has_high]).astype(jnp.int32)

    def move(x, pairs):
        return lax.ppermute(x, ("shot", "space"), pairs)

    def everywhere(space_pairs):
        return [(s * n + i, s * n + j) for s in range(shots) for i, j in space_pairs]

    def level_swap(parity):
        out = []
        for s in range(shots):
            for lv in range(levels):
                up = lv % 2 == parity
                to = lv + 1 if up else lv - 1
                for i in range(2):
                    at = 2 * lv + i
                    out.append((s * n + at, s * n + 2 * to + i if 0 <= to < levels else (s ^ 1) * n + at))
        return out

    swap_y = everywhere([(i, i ^ 1) for i in range(n)])
    swap_core = [(s * n + i, (s ^ 1) * n + i) for s in range(shots) for i in range(n)]
    swap_x = [(s * n + i, (s ^ 2) * n + i) for s in range(shots) for i in range(n)]
    swap_a, swap_b = level_swap(0), level_swap(1)
    near_a, near_b = [[(i, j) for i, j in p if i // n == j // n] for p in (swap_a, swap_b)]

    def after(x, *others):
        return lax.optimization_barrier((x, *others))[0]

    number = me * width + jnp.arange(width, dtype=jnp.int32)
    live = jnp.where(number < trace_counts[0], 1.0, 0.0)
    code = (owners[0, :, 0] * (length * ny) + surface_cells[0]).astype(F32)
    gathered = jnp.concatenate([traces * live[None], code[None], jnp.zeros((16 - steps - 1, width), F32)], 0)[None]
    reach = 2
    while reach < n:
        gathered = jnp.concatenate([gathered, move(gathered, everywhere([(i, i ^ reach) for i in range(n)]))], 0)
        if reach == 2:
            early = gathered
        reach *= 2

    half = length // 2
    plane = lambda k: VM((k, ny, nz), F32)
    edge, rest = pl.pallas_call(
        pack_kernel,
        out_shape=[plane(length), plane(length)],
        in_specs=[pl.BlockSpec(memory_space=pltpu.SMEM)] + [pl.BlockSpec(memory_space=pl.ANY)] * 2,
        out_specs=[pl.BlockSpec(memory_space=VM)] * 2,
        scratch_shapes=[pltpu.SemaphoreType.DMA((4,))],
        compiler_params=pltpu.CompilerParams(vmem_limit_bytes=LIMIT),
        name="pack",
    )(scal, *[pltpu.with_memory_space_constraint(x, pltpu.HBM) for x in (later, courant_sq)])
    y_cur = move(cur, swap_y)
    y_edge = move(after(edge, early), swap_y)
    y_rest = move(after(rest, early), swap_y)

    e, send_a, send_b = call(cur_kernel, [plane(32), plane(8), plane(8)], [scal, cur, after(y_cur, gathered)], free=(1,), name="field")
    recv_a, recv_b = move(send_a, near_a), move(send_b, near_b)
    gathered = jnp.concatenate([gathered, move(after(gathered, recv_b), swap_y)], 0)
    edge_a, edge_b = call(edge_kernel, [plane(8), plane(8)], [scal, edge, y_edge], name="edges")
    edge_a, edge_b = move(edge_a, swap_a), move(edge_b, swap_b)
    q = call(
        functools.partial(q_kernel, steps=steps, length=length),
        VM((3, ny, 128), F32),
        [scal, gathered],
        name="receivers",
    )
    o, a, c, wz, wy = call(
        model_kernel,
        [plane(24), plane(24), plane(24), VM((2 * nz, nz), BF16), VM((4 * ny, 8 * ny), BF16)],
        [scal, courant_sq, later, y_edge, y_rest],
        free=(1, 2),
        name="model",
    )
    g = jnp.zeros((length, ny, nz), F32)
    work = 2 * 16 * ny * nz * 60
    rounds = steps // 2
    for r in range(rounds):
        if r:
            recv_a = move(send_a, swap_a)
            recv_b = move(send_b, swap_b)
        if r:
            o, g = call(
                functools.partial(inner_kernel, r=r, length=length),
                [plane(24), plane(length)],
                [scal, e, o, a, c, q, wz, wy, forward, g],
                {2: 0, 9: 1},
                flops=work,
                name=f"inner{r}",
            )
        else:
            e, o = call(
                start_kernel,
                [plane(32), plane(24)],
                [scal, recv_a, recv_b, e, o, a, c, q, wz, wy],
                {3: 0, 4: 1},
                flops=work,
                name="start",
            )
        last = r == rounds - 1
        sent = []
        for side in "ab":
            got = {"a": recv_a, "b": recv_b}[side] if r else {"a": edge_a, "b": edge_b}[side]
            kept = 2 if r else 4
            outs = [plane(32), plane(24), plane(24), plane(24)][:kept] + ([] if last else [plane(8)])
            e, o, *new = call(
                functools.partial(side_kernel, r=r, side=side, last=last),
                outs,
                [scal, got, e, o, a, c, q, wz, wy],
                {2 + i: i for i in range(kept)},
                flops=work,
                name=f"side_{side}{r}",
            )
            if r == 0:
                a, c, *new = new
            sent += new
        if not last:
            send_a, send_b = sent

    part = ny // 4
    shares = [scal, e, o, forward, g]
    share = VM((length, 2 * part, nz), F32)
    give = call(functools.partial(share_kernel, steps=steps, give=True), [share], shares, name="give")[0]
    recv = move(give, swap_core)
    keep = call(functools.partial(share_kernel, steps=steps, give=False), [share], shares, name="keep")[0]
    give = call(pair_kernel, [VM((length, part, nz), F32)], [scal, keep, recv], name="pair")[0]
    last = move(give, swap_x)
    field, mine = call(
        own_kernel,
        [jax.ShapeDtypeStruct((length, ny, nz), F32), VM((length, part, nz), F32)],
        [scal, e, keep, recv, give],
        flops=work,
        name="own",
    )
    return field[None], mine + last


def solution(mesh):
    placed = (
        P("shot", None, "space"),
        P("shot", "space", None),
        P("shot", "space"),
        P("shot"),
        P("shot", "space", None, None),
        P("shot", "space", None, None),
        P("shot", None, "space", None, None),
        P("space", None, None),
    )
    return jax.shard_map(
        shards,
        mesh=mesh,
        in_specs=placed,
        out_specs=(P("shot", "space", None, None), P("space", "shot", None)),
        check_vma=False,
    )
```

```python
import functools

import jax
import jax.numpy as jnp
from jax import lax
from jax.experimental import pallas as pl
from jax.experimental.pallas import tpu as pltpu
from jax.sharding import PartitionSpec as P

SCALE = 5040.0
TAPS = (8064.0, -1008.0, 128.0, -9.0)
CENTRE = 3.0 * (-205.0 / 72.0)

LIMIT = 16 * 1024 * 1024
VM = pltpu.VMEM
F32 = jnp.float32
BF16 = jnp.bfloat16


def vmem(x):
    return pltpu.with_memory_space_constraint(x, VM)


def band(rows, cols, block):
    r = lax.broadcasted_iota(jnp.int32, (rows, cols), 0)
    c = lax.broadcasted_iota(jnp.int32, (rows, cols), 1)
    r = r % cols
    c = c % rows
    gap = jnp.abs(r - c)
    out = jnp.zeros((rows, cols), F32)
    for j, w in enumerate(TAPS):
        out = jnp.where(gap == j + 1, w, out)
    return jnp.where(r // block == c // block, out, 0.0).astype(BF16)


def advance(src, so, prev, po, dst, do, a_ref, c_ref, q_ref, wz_ref, wy_ref, start, groups, k, extra=None):
    ny, nz = src.shape[1], src.shape[2]
    half = q_ref.shape[2]
    lane = lax.broadcasted_iota(jnp.int32, (ny, half), 1)
    for g in range(groups):
        t = start + 4 * g
        v = src[t + so : t + so + 4].reshape(4 * ny, nz)
        hi = v.astype(BF16)
        lo = (v - hi.astype(F32)).astype(BF16)
        s = jnp.dot(jnp.concatenate([hi, lo], 1), wz_ref[...], preferred_element_type=F32)
        s = s + jnp.dot(wy_ref[...], jnp.concatenate([hi, lo], 0), preferred_element_type=F32)
        for i in range(4):
            p = t + i
            total = s[i * ny : (i + 1) * ny]
            for j, w in enumerate(TAPS):
                total = total + w * (src[p + so + j + 1] + src[p + so - j - 1])
            fresh = a_ref[p + 4] * src[p + so] - prev[p + po] + c_ref[p + 4] * total
            x = p + 4
            shift = (2 - ((x % 8) * 16 + k)) % half
            q = q_ref[x // 8]
            q = jnp.where(lane == 2, pltpu.roll(q, shift, 1), 0.0)
            fresh = jnp.concatenate([fresh[:, :half] + q, fresh[:, half:]], 1)
            dst[p + do] = fresh
            if extra is not None:
                extra[p - start] = fresh


def local_of(scal_ref, g, length):
    return jnp.where(scal_ref[1] == 1, 2 * length - 1 - g, g)


def q_kernel(scal_ref, gathered_ref, q_ref, *, steps, length):
    n, rows, width = gathered_ref.shape
    across = q_ref.shape[1]
    level, odd = scal_ref[0], scal_ref[1]
    x_iota = lax.broadcasted_iota(jnp.int32, (8, 16, width), 0)
    y_iota = lax.broadcasted_iota(jnp.int32, (across, width), 0)

    def body(b, acc):
        block = gathered_ref[b]
        code = block[steps : steps + 1].astype(jnp.int32)
        gx = code // across
        y = code - gx * across
        gx = gx - level * (2 * length)
        x = jnp.where(odd == 1, 2 * length - 1 - gx, gx) + 4
        one_y = jnp.where(y_iota == y, 1.0, 0.0).astype(BF16)
        out = []
        for j in range(3):
            t = jnp.where(x_iota + 8 * j == x[None], block[None], 0.0).reshape(8 * 16, width)
            hi = t.astype(BF16)
            lo = (t - hi.astype(F32)).astype(BF16)
            dims = (((1,), (1,)), ((), ()))
            o = lax.dot_general(one_y, hi, dims, preferred_element_type=F32)
            o = o + lax.dot_general(one_y, lo, dims, preferred_element_type=F32)
            out.append(acc[j] + o)
        return tuple(out)

    zero = jnp.zeros(q_ref.shape[1:], F32)
    acc = lax.fori_loop(0, n, body, (zero, zero, zero), unroll=4)
    for j in range(3):
        q_ref[j] = acc[j]


def keep_if(flag, x):
    return jnp.where(flag == 1, x, 0.0)


def pack_kernel(scal_ref, later_ref, c_ref, edge_ref, rest_ref, sems):
    half = edge_ref.shape[0] // 2
    y = scal_ref[2]
    copies = []
    for out, at in ((edge_ref, half * y), (rest_ref, half * (1 - y))):
        for i, src in enumerate((later_ref, c_ref)):
            copies.append((src.at[pl.ds(at, half)], out.at[i * half : (i + 1) * half]))
    copies = [pltpu.make_async_copy(src, dst, sems.at[i]) for i, (src, dst) in enumerate(copies)]
    for copy in copies:
        copy.start()
    for copy in copies:
        copy.wait()


def cur_kernel(scal_ref, own, other, e_ref, send_a, send_b):
    length = own.shape[0]
    y = scal_ref[2]
    for p in range(length):
        e_ref[local_of(scal_ref, y * length + p, length) + 8] = own[p]
        e_ref[local_of(scal_ref, (1 - y) * length + p, length) + 8] = other[p]
    send_a[...] = e_ref[16:24]
    send_b[...] = e_ref[8:16]


def edge_kernel(scal_ref, own, other, send_a, send_b):
    half = own.shape[0] // 2
    odd = scal_ref[1]

    def put(dst, src):
        for p in range(half):
            at = jnp.where(odd == 1, half - 1 - p, p)
            dst[at] = src[p]
            dst[half + at] = src[half + p]

    def split(a, b):
        put(send_a, a)
        put(send_b, b)

    own_a = (odd + scal_ref[2]) % 2
    pl.when(own_a == 1)(lambda: split(own, other))
    pl.when(own_a == 0)(lambda: split(other, own))


def model_kernel(scal_ref, c_own, lat_own, edge, rest, o_ref, a_ref, c_ref, wz_ref, wy_ref):
    length, ny, nz = c_own.shape
    half = length // 2
    y = scal_ref[2]

    def put(g, later, cv):
        j = local_of(scal_ref, g, length) + 4
        o_ref[j] = later
        c_ref[j] = cv * (1.0 / SCALE)
        a_ref[j] = 2.0 + CENTRE * cv

    for p in range(length):
        put(y * length + p, lat_own[p], c_own[p])
    base = (1 - y) * length
    for p in range(half):
        put(base + half * (1 - y) + p, edge[p], edge[half + p])
        put(base + half * y + p, rest[p], rest[half + p])
    wz_ref[...] = band(2 * nz, nz, nz)
    wy_ref[...] = band(4 * ny, 8 * ny, ny)


def start_kernel(scal_ref, recv_a, recv_b, e_in, o_in, a_ref, c_ref, q_ref, wz_ref, wy_ref, e_ref, o_ref):
    odd = scal_ref[1]
    for i in range(8):
        e_ref[24 + i] = keep_if(scal_ref[6 - odd], recv_a[7 - i])
        e_ref[7 - i] = keep_if(scal_ref[5 + odd], recv_b[i])
    advance(e_ref, 8, o_ref, 4, o_ref, 4, a_ref, c_ref, q_ref, wz_ref, wy_ref, 0, 4, 0)


def inner_kernel(scal_ref, e_ref, o_in, a_ref, c_ref, q_ref, wz_ref, wy_ref, f_ref, g_in, o_ref, g_ref, *, r, length):
    y = scal_ref[2]
    if r > 0:
        for p in range(length):
            j = local_of(scal_ref, y * length + p, length)
            add = o_ref[j + 4] * f_ref[2 * r - 2, p].astype(F32) + e_ref[j + 8] * f_ref[2 * r - 1, p].astype(F32)
            g_ref[p] = add if r == 1 else g_ref[p] + add
    advance(e_ref, 8, o_ref, 4, o_ref, 4, a_ref, c_ref, q_ref, wz_ref, wy_ref, 4, 2, 2 * r)


def side_kernel(scal_ref, recv_ref, e_in, o_in, a_in, c_in, q_ref, wz_ref, wy_ref, e_ref, o_ref, *outs, r, side, last):
    if r == 0:
        a_ref, c_ref, new = outs
    else:
        a_ref, c_ref, new = a_in, c_in, None if last else outs[0]

    def work():
        odd = scal_ref[1]
        inside = scal_ref[6 - odd] if side == "a" else scal_ref[5 + odd]
        args = (a_ref, c_ref, q_ref, wz_ref, wy_ref)
        if r == 0:
            for i in range(4):
                to, at = (20 + i, 3 - i) if side == "a" else (3 - i, i)
                o_ref[to] = keep_if(inside, recv_ref[at])
                cv = keep_if(inside, recv_ref[4 + at])
                c_ref[to] = cv * (1.0 / SCALE)
                a_ref[to] = 2.0 + CENTRE * cv
            advance(e_ref, 8, o_ref, 4, o_ref, 4, *args, 16 if side == "a" else -4, 1, 0)
        else:
            for i in range(8):
                if side == "a":
                    e_ref[24 + i] = keep_if(inside, recv_ref[7 - i])
                else:
                    e_ref[7 - i] = keep_if(inside, recv_ref[i])
            advance(e_ref, 8, o_ref, 4, o_ref, 4, *args, 12 if side == "a" else -4, 2, 2 * r)
        advance(o_ref, 4, e_ref, 8, e_ref, 8, *args, 8 if side == "a" else 0, 2, 2 * r + 1, extra=new)

    if last:
        own_a = (scal_ref[1] + scal_ref[2]) % 2
        pl.when(own_a == (1 if side == "a" else 0))(work)
    else:
        work()


def share_kernel(scal_ref, e_ref, o_ref, f_ref, g_in, g_ref, *, steps, give):
    length, rows, _ = g_ref.shape
    part = rows // 2
    y, core = scal_ref[2], scal_ref[3]
    mine = 1 - core if give else core
    for p in range(length):
        j = local_of(scal_ref, y * length + p, length)
        for x in range(2):
            at = pl.ds(pl.multiple_of(part * (2 * x + mine), part), part)
            g_ref[p, x * part : (x + 1) * part] = (
                g_in[p, at]
                + o_ref[j + 4, at] * f_ref[steps - 2, p, at].astype(F32)
                + e_ref[j + 8, at] * f_ref[steps - 1, p, at].astype(F32)
            )


def pair_kernel(scal_ref, keep_ref, recv_ref, give_ref):
    x = scal_ref[4]
    part = give_ref.shape[1]
    at = pl.ds(pl.multiple_of(part * (1 - x), part), part)
    for p in range(keep_ref.shape[0]):
        give_ref[p] = keep_ref[p, at] + recv_ref[p, at]


def own_kernel(scal_ref, e_ref, keep_ref, recv_ref, late_ref, field_ref, mine_ref):
    x = scal_ref[4]
    length, part, _ = mine_ref.shape
    at = pl.ds(pl.multiple_of(part * x, part), part)
    for p in range(length):
        field_ref[p] = e_ref[local_of(scal_ref, scal_ref[2] * length + p, length) + 8]
        mine_ref[p] = keep_ref[p, at] + recv_ref[p, at]


def call(kernel, out_shapes, args, aliases=None, free=(), flops=0, name=None):
    smem = pl.BlockSpec(memory_space=pltpu.SMEM)
    vm = pl.BlockSpec(memory_space=VM)
    specs = [smem if a.dtype == jnp.int32 and a.ndim == 1 else vm for a in args]
    args = [a if s is smem or i in free else vmem(a) for i, (a, s) in enumerate(zip(args, specs))]
    return pl.pallas_call(
        kernel,
        out_shape=out_shapes,
        in_specs=specs,
        out_specs=jax.tree.map(lambda _: vm, out_shapes),
        input_output_aliases=aliases or {},
        compiler_params=pltpu.CompilerParams(vmem_limit_bytes=LIMIT),
        cost_estimate=pl.CostEstimate(flops=flops, bytes_accessed=1 << 20, transcendentals=0),
        name=name,
    )(*args)


def shards(residual_traces, owners, surface_cells, trace_counts, start_current, start_later, forward_accel, courant_sq):
    traces = residual_traces[0]
    forward = forward_accel[0]
    cur, later = start_current[0], start_later[0]
    length, ny, nz = courant_sq.shape
    steps, width = traces.shape
    n, shots = lax.axis_size("space"), lax.axis_size("shot")
    levels = n // 2
    me, shot = lax.axis_index("space"), lax.axis_index("shot")
    level, y, core = me // 2, me % 2, shot % 2
    has_low = jnp.where(level > 0, 1, 0)
    has_high = jnp.where(level < levels - 1, 1, 0)
    scal = jnp.stack([level, level % 2, y, core, shot // 2, has_low, has_high]).astype(jnp.int32)

    def move(x, pairs):
        return lax.ppermute(x, ("shot", "space"), pairs)

    def everywhere(space_pairs):
        return [(s * n + i, s * n + j) for s in range(shots) for i, j in space_pairs]

    def level_swap(parity):
        out = []
        for s in range(shots):
            for lv in range(levels):
                up = lv % 2 == parity
                to = lv + 1 if up else lv - 1
                for i in range(2):
                    at = 2 * lv + i
                    out.append((s * n + at, s * n + 2 * to + i if 0 <= to < levels else (s ^ 1) * n + at))
        return out

    swap_y = everywhere([(i, i ^ 1) for i in range(n)])
    swap_core = [(s * n + i, (s ^ 1) * n + i) for s in range(shots) for i in range(n)]
    swap_x = [(s * n + i, (s ^ 2) * n + i) for s in range(shots) for i in range(n)]
    swap_a, swap_b = level_swap(0), level_swap(1)
    near_a, near_b = [[(i, j) for i, j in p if i // n == j // n] for p in (swap_a, swap_b)]

    def after(x, *others):
        return lax.optimization_barrier((x, *others))[0]

    number = me * width + jnp.arange(width, dtype=jnp.int32)
    live = jnp.where(number < trace_counts[0], 1.0, 0.0)
    code = (owners[0, :, 0] * (length * ny) + surface_cells[0]).astype(F32)
    gathered = jnp.concatenate([traces * live[None], code[None], jnp.zeros((16 - steps - 1, width), F32)], 0)[None]
    reach = 2
    while reach < n:
        gathered = jnp.concatenate([gathered, move(gathered, everywhere([(i, i ^ reach) for i in range(n)]))], 0)
        if reach == 2:
            early = gathered
        reach *= 2

    half = length // 2
    plane = lambda k: VM((k, ny, nz), F32)
    edge, rest = pl.pallas_call(
        pack_kernel,
        out_shape=[plane(length), plane(length)],
        in_specs=[pl.BlockSpec(memory_space=pltpu.SMEM)] + [pl.BlockSpec(memory_space=pl.ANY)] * 2,
        out_specs=[pl.BlockSpec(memory_space=VM)] * 2,
        scratch_shapes=[pltpu.SemaphoreType.DMA((4,))],
        compiler_params=pltpu.CompilerParams(vmem_limit_bytes=LIMIT),
        name="pack",
    )(scal, *[pltpu.with_memory_space_constraint(x, pltpu.HBM) for x in (later, courant_sq)])
    y_cur = move(cur, swap_y)
    y_edge = move(after(edge, early), swap_y)
    y_rest = move(after(rest, early), swap_y)

    e, send_a, send_b = call(cur_kernel, [plane(32), plane(8), plane(8)], [scal, cur, y_cur], free=(1,), name="field")
    recv_a, recv_b = move(send_a, near_a), move(send_b, near_b)
    gathered = jnp.concatenate([gathered, move(after(gathered, recv_b), swap_y)], 0)
    edge_a, edge_b = call(edge_kernel, [plane(8), plane(8)], [scal, edge, y_edge], name="edges")
    edge_a, edge_b = move(edge_a, swap_a), move(edge_b, swap_b)
    q = call(
        functools.partial(q_kernel, steps=steps, length=length),
        VM((3, ny, 128), F32),
        [scal, gathered],
        name="receivers",
    )
    o, a, c, wz, wy = call(
        model_kernel,
        [plane(24), plane(24), plane(24), VM((2 * nz, nz), BF16), VM((4 * ny, 8 * ny), BF16)],
        [scal, courant_sq, later, y_edge, y_rest],
        free=(1, 2),
        name="model",
    )
    g = jnp.zeros((length, ny, nz), F32)
    work = 2 * 16 * ny * nz * 60
    rounds = steps // 2
    for r in range(rounds):
        if r:
            recv_a = move(send_a, swap_a)
            recv_b = move(send_b, swap_b)
        if r:
            o, g = call(
                functools.partial(inner_kernel, r=r, length=length),
                [plane(24), plane(length)],
                [scal, e, o, a, c, q, wz, wy, forward, g],
                {2: 0, 9: 1},
                flops=work,
                name=f"inner{r}",
            )
        else:
            e, o = call(
                start_kernel,
                [plane(32), plane(24)],
                [scal, recv_a, recv_b, e, o, a, c, q, wz, wy],
                {3: 0, 4: 1},
                flops=work,
                name="start",
            )
        last = r == rounds - 1
        sent = []
        for side in "ab":
            got = {"a": recv_a, "b": recv_b}[side] if r else {"a": edge_a, "b": edge_b}[side]
            kept = 2 if r else 4
            outs = [plane(32), plane(24), plane(24), plane(24)][:kept] + ([] if last else [plane(8)])
            e, o, *new = call(
                functools.partial(side_kernel, r=r, side=side, last=last),
                outs,
                [scal, got, e, o, a, c, q, wz, wy],
                {2 + i: i for i in range(kept)},
                flops=work,
                name=f"side_{side}{r}",
            )
            if r == 0:
                a, c, *new = new
            sent += new
        if not last:
            send_a, send_b = sent

    part = ny // 4
    shares = [scal, e, o, forward, g]
    share = VM((length, 2 * part, nz), F32)
    give = call(functools.partial(share_kernel, steps=steps, give=True), [share], shares, name="give")[0]
    recv = move(give, swap_core)
    keep = call(functools.partial(share_kernel, steps=steps, give=False), [share], shares, name="keep")[0]
    give = call(pair_kernel, [VM((length, part, nz), F32)], [scal, keep, recv], name="pair")[0]
    last = move(give, swap_x)
    field, mine = call(
        own_kernel,
        [jax.ShapeDtypeStruct((length, ny, nz), F32), VM((length, part, nz), F32)],
        [scal, e, keep, recv, give],
        flops=work,
        name="own",
    )
    return field[None], mine + last


def solution(mesh):
    placed = (
        P("shot", None, "space"),
        P("shot", "space", None),
        P("shot", "space"),
        P("shot"),
        P("shot", "space", None, None),
        P("shot", "space", None, None),
        P("shot", None, "space", None, None),
        P("space", None, None),
    )
    return jax.shard_map(
        shards,
        mesh=mesh,
        in_specs=placed,
        out_specs=(P("shot", "space", None, None), P("space", "shot", None)),
        check_vma=False,
    )
```

```python
import functools

import jax
import jax.numpy as jnp
from jax import lax
from jax.experimental import pallas as pl
from jax.experimental.pallas import tpu as pltpu
from jax.sharding import PartitionSpec as P

SCALE = 5040.0
TAPS = (8064.0, -1008.0, 128.0, -9.0)
CENTRE = 3.0 * (-205.0 / 72.0)

LIMIT = 16 * 1024 * 1024
VM = pltpu.VMEM
F32 = jnp.float32
BF16 = jnp.bfloat16


def vmem(x):
    return pltpu.with_memory_space_constraint(x, VM)


def band(rows, cols, block):
    r = lax.broadcasted_iota(jnp.int32, (rows, cols), 0)
    c = lax.broadcasted_iota(jnp.int32, (rows, cols), 1)
    r = r % cols
    c = c % rows
    gap = jnp.abs(r - c)
    out = jnp.zeros((rows, cols), F32)
    for j, w in enumerate(TAPS):
        out = jnp.where(gap == j + 1, w, out)
    return jnp.where(r // block == c // block, out, 0.0).astype(BF16)


def advance(src, so, prev, po, dst, do, a_ref, c_ref, q_ref, wz_ref, wy_ref, start, groups, k, extra=None):
    ny, nz = src.shape[1], src.shape[2]
    half = q_ref.shape[2]
    lane = lax.broadcasted_iota(jnp.int32, (ny, half), 1)
    for g in range(groups):
        t = start + 4 * g
        v = src[t + so : t + so + 4].reshape(4 * ny, nz)
        hi = v.astype(BF16)
        lo = (v - hi.astype(F32)).astype(BF16)
        s = jnp.dot(jnp.concatenate([hi, lo], 1), wz_ref[...], preferred_element_type=F32)
        s = s + jnp.dot(wy_ref[...], jnp.concatenate([hi, lo], 0), preferred_element_type=F32)
        for i in range(4):
            p = t + i
            total = s[i * ny : (i + 1) * ny]
            for j, w in enumerate(TAPS):
                total = total + w * (src[p + so + j + 1] + src[p + so - j - 1])
            fresh = a_ref[p + 4] * src[p + so] - prev[p + po] + c_ref[p + 4] * total
            x = p + 4
            shift = (2 - ((x % 8) * 16 + k)) % half
            q = q_ref[x // 8]
            q = jnp.where(lane == 2, pltpu.roll(q, shift, 1), 0.0)
            fresh = jnp.concatenate([fresh[:, :half] + q, fresh[:, half:]], 1)
            dst[p + do] = fresh
            if extra is not None:
                extra[p - start] = fresh


def local_of(scal_ref, g, length):
    return jnp.where(scal_ref[1] == 1, 2 * length - 1 - g, g)


def q_kernel(scal_ref, gathered_ref, q_ref, *, steps, length):
    n, rows, width = gathered_ref.shape
    across = q_ref.shape[1]
    level, odd = scal_ref[0], scal_ref[1]
    x_iota = lax.broadcasted_iota(jnp.int32, (8, 16, width), 0)
    y_iota = lax.broadcasted_iota(jnp.int32, (across, width), 0)

    def body(b, acc):
        block = gathered_ref[b]
        code = block[steps : steps + 1].astype(jnp.int32)
        gx = code // across
        y = code - gx * across
        gx = gx - level * (2 * length)
        x = jnp.where(odd == 1, 2 * length - 1 - gx, gx) + 4
        one_y = jnp.where(y_iota == y, 1.0, 0.0).astype(BF16)
        out = []
        for j in range(3):
            t = jnp.where(x_iota + 8 * j == x[None], block[None], 0.0).reshape(8 * 16, width)
            hi = t.astype(BF16)
            lo = (t - hi.astype(F32)).astype(BF16)
            dims = (((1,), (1,)), ((), ()))
            o = lax.dot_general(one_y, hi, dims, preferred_element_type=F32)
            o = o + lax.dot_general(one_y, lo, dims, preferred_element_type=F32)
            out.append(acc[j] + o)
        return tuple(out)

    zero = jnp.zeros(q_ref.shape[1:], F32)
    acc = lax.fori_loop(0, n, body, (zero, zero, zero), unroll=4)
    for j in range(3):
        q_ref[j] = acc[j]


def keep_if(flag, x):
    return jnp.where(flag == 1, x, 0.0)


def pack_kernel(scal_ref, later_ref, c_ref, edge_ref, rest_ref, sems):
    half = edge_ref.shape[0] // 2
    y = scal_ref[2]
    copies = []
    for out, at in ((edge_ref, half * y), (rest_ref, half * (1 - y))):
        for i, src in enumerate((later_ref, c_ref)):
            copies.append((src.at[pl.ds(at, half)], out.at[i * half : (i + 1) * half]))
    copies = [pltpu.make_async_copy(src, dst, sems.at[i]) for i, (src, dst) in enumerate(copies)]
    for copy in copies:
        copy.start()
    for copy in copies:
        copy.wait()


def cur_kernel(scal_ref, own, other, e_ref, send_a, send_b):
    length = own.shape[0]
    y = scal_ref[2]
    for p in range(length):
        e_ref[local_of(scal_ref, y * length + p, length) + 8] = own[p]
        e_ref[local_of(scal_ref, (1 - y) * length + p, length) + 8] = other[p]
    send_a[...] = e_ref[16:24]
    send_b[...] = e_ref[8:16]


def edge_kernel(scal_ref, own, other, send_a, send_b):
    half = own.shape[0] // 2
    odd = scal_ref[1]

    def put(dst, src):
        for p in range(half):
            at = jnp.where(odd == 1, half - 1 - p, p)
            dst[at] = src[p]
            dst[half + at] = src[half + p]

    def split(a, b):
        put(send_a, a)
        put(send_b, b)

    own_a = (odd + scal_ref[2]) % 2
    pl.when(own_a == 1)(lambda: split(own, other))
    pl.when(own_a == 0)(lambda: split(other, own))


def model_kernel(scal_ref, c_own, lat_own, edge, rest, o_ref, a_ref, c_ref, wz_ref, wy_ref):
    length, ny, nz = c_own.shape
    half = length // 2
    y = scal_ref[2]

    def put(g, later, cv):
        j = local_of(scal_ref, g, length) + 4
        o_ref[j] = later
        c_ref[j] = cv * (1.0 / SCALE)
        a_ref[j] = 2.0 + CENTRE * cv

    for p in range(length):
        put(y * length + p, lat_own[p], c_own[p])
    base = (1 - y) * length
    for p in range(half):
        put(base + half * (1 - y) + p, edge[p], edge[half + p])
        put(base + half * y + p, rest[p], rest[half + p])
    wz_ref[...] = band(2 * nz, nz, nz)
    wy_ref[...] = band(4 * ny, 8 * ny, ny)


def start_kernel(scal_ref, recv_a, recv_b, e_in, o_in, a_ref, c_ref, q_ref, wz_ref, wy_ref, e_ref, o_ref):
    odd = scal_ref[1]
    for i in range(8):
        e_ref[24 + i] = keep_if(scal_ref[6 - odd], recv_a[7 - i])
        e_ref[7 - i] = keep_if(scal_ref[5 + odd], recv_b[i])
    advance(e_ref, 8, o_ref, 4, o_ref, 4, a_ref, c_ref, q_ref, wz_ref, wy_ref, 0, 4, 0)


def inner_kernel(scal_ref, e_ref, o_in, a_ref, c_ref, q_ref, wz_ref, wy_ref, f_ref, g_in, o_ref, g_ref, *, r, length):
    y = scal_ref[2]
    if r > 0:
        for p in range(length):
            j = local_of(scal_ref, y * length + p, length)
            add = o_ref[j + 4] * f_ref[2 * r - 2, p].astype(F32) + e_ref[j + 8] * f_ref[2 * r - 1, p].astype(F32)
            g_ref[p] = add if r == 1 else g_ref[p] + add
    advance(e_ref, 8, o_ref, 4, o_ref, 4, a_ref, c_ref, q_ref, wz_ref, wy_ref, 4, 2, 2 * r)


def side_kernel(scal_ref, recv_ref, e_in, o_in, a_in, c_in, q_ref, wz_ref, wy_ref, e_ref, o_ref, *outs, r, side, last):
    if r == 0:
        a_ref, c_ref, new = outs
    else:
        a_ref, c_ref, new = a_in, c_in, None if last else outs[0]

    def work():
        odd = scal_ref[1]
        inside = scal_ref[6 - odd] if side == "a" else scal_ref[5 + odd]
        args = (a_ref, c_ref, q_ref, wz_ref, wy_ref)
        if r == 0:
            for i in range(4):
                to, at = (20 + i, 3 - i) if side == "a" else (3 - i, i)
                o_ref[to] = keep_if(inside, recv_ref[at])
                cv = keep_if(inside, recv_ref[4 + at])
                c_ref[to] = cv * (1.0 / SCALE)
                a_ref[to] = 2.0 + CENTRE * cv
            advance(e_ref, 8, o_ref, 4, o_ref, 4, *args, 16 if side == "a" else -4, 1, 0)
        else:
            for i in range(8):
                if side == "a":
                    e_ref[24 + i] = keep_if(inside, recv_ref[7 - i])
                else:
                    e_ref[7 - i] = keep_if(inside, recv_ref[i])
            advance(e_ref, 8, o_ref, 4, o_ref, 4, *args, 12 if side == "a" else -4, 2, 2 * r)
        advance(o_ref, 4, e_ref, 8, e_ref, 8, *args, 8 if side == "a" else 0, 2, 2 * r + 1, extra=new)

    if last:
        own_a = (scal_ref[1] + scal_ref[2]) % 2
        pl.when(own_a == (1 if side == "a" else 0))(work)
    else:
        work()


def share_kernel(scal_ref, e_ref, o_ref, f_ref, g_in, g_ref, *, steps, give):
    length, rows, _ = g_ref.shape
    part = rows // 2
    y, core = scal_ref[2], scal_ref[3]
    mine = 1 - core if give else core
    for p in range(length):
        j = local_of(scal_ref, y * length + p, length)
        for x in range(2):
            at = pl.ds(pl.multiple_of(part * (2 * x + mine), part), part)
            g_ref[p, x * part : (x + 1) * part] = (
                g_in[p, at]
                + o_ref[j + 4, at] * f_ref[steps - 2, p, at].astype(F32)
                + e_ref[j + 8, at] * f_ref[steps - 1, p, at].astype(F32)
            )


def last_kernel(scal_ref, recv_ref, *refs, r, steps):
    state, (f_ref, g_in, e_ref, o_ref, give_ref) = refs[:7], refs[7:]
    side_kernel(scal_ref, recv_ref, *state, e_ref, o_ref, r=r, side="b", last=True)
    share_kernel(scal_ref, e_ref, o_ref, f_ref, g_in, give_ref, steps=steps, give=True)


def pair_kernel(scal_ref, keep_ref, recv_ref, give_ref):
    x = scal_ref[4]
    part = give_ref.shape[1]
    at = pl.ds(pl.multiple_of(part * (1 - x), part), part)
    for p in range(keep_ref.shape[0]):
        give_ref[p] = keep_ref[p, at] + recv_ref[p, at]


def own_kernel(scal_ref, e_ref, keep_ref, recv_ref, late_ref, field_ref, mine_ref):
    x = scal_ref[4]
    length, part, _ = mine_ref.shape
    at = pl.ds(pl.multiple_of(part * x, part), part)
    for p in range(length):
        field_ref[p] = e_ref[local_of(scal_ref, scal_ref[2] * length + p, length) + 8]
        mine_ref[p] = keep_ref[p, at] + recv_ref[p, at]


def call(kernel, out_shapes, args, aliases=None, free=(), flops=0, name=None):
    smem = pl.BlockSpec(memory_space=pltpu.SMEM)
    vm = pl.BlockSpec(memory_space=VM)
    specs = [smem if a.dtype == jnp.int32 and a.ndim == 1 else vm for a in args]
    args = [a if s is smem or i in free else vmem(a) for i, (a, s) in enumerate(zip(args, specs))]
    return pl.pallas_call(
        kernel,
        out_shape=out_shapes,
        in_specs=specs,
        out_specs=jax.tree.map(lambda _: vm, out_shapes),
        input_output_aliases=aliases or {},
        compiler_params=pltpu.CompilerParams(vmem_limit_bytes=LIMIT),
        cost_estimate=pl.CostEstimate(flops=flops, bytes_accessed=1 << 20, transcendentals=0),
        name=name,
    )(*args)


def shards(residual_traces, owners, surface_cells, trace_counts, start_current, start_later, forward_accel, courant_sq):
    traces = residual_traces[0]
    forward = forward_accel[0]
    cur, later = start_current[0], start_later[0]
    length, ny, nz = courant_sq.shape
    steps, width = traces.shape
    n, shots = lax.axis_size("space"), lax.axis_size("shot")
    levels = n // 2
    me, shot = lax.axis_index("space"), lax.axis_index("shot")
    level, y, core = me // 2, me % 2, shot % 2
    has_low = jnp.where(level > 0, 1, 0)
    has_high = jnp.where(level < levels - 1, 1, 0)
    scal = jnp.stack([level, level % 2, y, core, shot // 2, has_low, has_high]).astype(jnp.int32)

    def move(x, pairs):
        return lax.ppermute(x, ("shot", "space"), pairs)

    def everywhere(space_pairs):
        return [(s * n + i, s * n + j) for s in range(shots) for i, j in space_pairs]

    def level_swap(parity):
        out = []
        for s in range(shots):
            for lv in range(levels):
                up = lv % 2 == parity
                to = lv + 1 if up else lv - 1
                for i in range(2):
                    at = 2 * lv + i
                    out.append((s * n + at, s * n + 2 * to + i if 0 <= to < levels else (s ^ 1) * n + at))
        return out

    swap_y = everywhere([(i, i ^ 1) for i in range(n)])
    swap_core = [(s * n + i, (s ^ 1) * n + i) for s in range(shots) for i in range(n)]
    swap_x = [(s * n + i, (s ^ 2) * n + i) for s in range(shots) for i in range(n)]
    swap_a, swap_b = level_swap(0), level_swap(1)
    near_a, near_b = [[(i, j) for i, j in p if i // n == j // n] for p in (swap_a, swap_b)]

    def after(x, *others):
        return lax.optimization_barrier((x, *others))[0]

    number = me * width + jnp.arange(width, dtype=jnp.int32)
    live = jnp.where(number < trace_counts[0], 1.0, 0.0)
    code = (owners[0, :, 0] * (length * ny) + surface_cells[0]).astype(F32)
    gathered = jnp.concatenate([traces * live[None], code[None], jnp.zeros((16 - steps - 1, width), F32)], 0)[None]
    reach = 2
    while reach < n:
        gathered = jnp.concatenate([gathered, move(gathered, everywhere([(i, i ^ reach) for i in range(n)]))], 0)
        if reach == 2:
            early = gathered
        reach *= 2

    half = length // 2
    plane = lambda k: VM((k, ny, nz), F32)
    edge, rest = pl.pallas_call(
        pack_kernel,
        out_shape=[plane(length), plane(length)],
        in_specs=[pl.BlockSpec(memory_space=pltpu.SMEM)] + [pl.BlockSpec(memory_space=pl.ANY)] * 2,
        out_specs=[pl.BlockSpec(memory_space=VM)] * 2,
        scratch_shapes=[pltpu.SemaphoreType.DMA((4,))],
        compiler_params=pltpu.CompilerParams(vmem_limit_bytes=LIMIT),
        name="pack",
    )(scal, *[pltpu.with_memory_space_constraint(x, pltpu.HBM) for x in (later, courant_sq)])
    y_cur = move(cur, swap_y)
    y_edge = move(after(edge, early), swap_y)
    y_rest = move(after(rest, early), swap_y)

    e, send_a, send_b = call(cur_kernel, [plane(32), plane(8), plane(8)], [scal, cur, y_cur], free=(1,), name="field")
    recv_a, recv_b = move(send_a, near_a), move(send_b, near_b)
    gathered = jnp.concatenate([gathered, move(after(gathered, recv_b), swap_y)], 0)
    edge_a, edge_b = call(edge_kernel, [plane(8), plane(8)], [scal, edge, y_edge], name="edges")
    edge_a, edge_b = move(edge_a, swap_a), move(edge_b, swap_b)
    q = call(
        functools.partial(q_kernel, steps=steps, length=length),
        VM((3, ny, 128), F32),
        [scal, gathered],
        name="receivers",
    )
    o, a, c, wz, wy = call(
        model_kernel,
        [plane(24), plane(24), plane(24), VM((2 * nz, nz), BF16), VM((4 * ny, 8 * ny), BF16)],
        [scal, courant_sq, later, y_edge, y_rest],
        free=(1, 2),
        name="model",
    )
    g = jnp.zeros((length, ny, nz), F32)
    work = 2 * 16 * ny * nz * 60
    rounds = steps // 2
    for r in range(rounds):
        if r:
            recv_a = move(send_a, swap_a)
            recv_b = move(send_b, swap_b)
        if r:
            o, g = call(
                functools.partial(inner_kernel, r=r, length=length),
                [plane(24), plane(length)],
                [scal, e, o, a, c, q, wz, wy, forward, g],
                {2: 0, 9: 1},
                flops=work,
                name=f"inner{r}",
            )
        else:
            e, o = call(
                start_kernel,
                [plane(32), plane(24)],
                [scal, recv_a, recv_b, e, o, a, c, q, wz, wy],
                {3: 0, 4: 1},
                flops=work,
                name="start",
            )
        last = r == rounds - 1
        sent = []
        for side in "ab":
            if last and side == "b":
                e, o, give = call(
                    functools.partial(last_kernel, r=r, steps=steps),
                    [plane(32), plane(24), VM((length, ny // 2, nz), F32)],
                    [scal, recv_b, e, o, a, c, q, wz, wy, forward, g],
                    {2: 0, 3: 1},
                    flops=work,
                    name="last",
                )
                continue
            got = {"a": recv_a, "b": recv_b}[side] if r else {"a": edge_a, "b": edge_b}[side]
            kept = 2 if r else 4
            outs = [plane(32), plane(24), plane(24), plane(24)][:kept] + ([] if last else [plane(8)])
            e, o, *new = call(
                functools.partial(side_kernel, r=r, side=side, last=last),
                outs,
                [scal, got, e, o, a, c, q, wz, wy],
                {2 + i: i for i in range(kept)},
                flops=work,
                name=f"side_{side}{r}",
            )
            if r == 0:
                a, c, *new = new
            sent += new
        if not last:
            send_a, send_b = sent

    part = ny // 4
    shares = [scal, e, o, forward, g]
    share = VM((length, 2 * part, nz), F32)
    recv = move(give, swap_core)
    keep = call(functools.partial(share_kernel, steps=steps, give=False), [share], shares, name="keep")[0]
    give = call(pair_kernel, [VM((length, part, nz), F32)], [scal, keep, recv], name="pair")[0]
    last = move(give, swap_x)
    field, mine = call(
        own_kernel,
        [jax.ShapeDtypeStruct((length, ny, nz), F32), VM((length, part, nz), F32)],
        [scal, e, keep, recv, give],
        flops=work,
        name="own",
    )
    return field[None], mine + last


def solution(mesh):
    placed = (
        P("shot", None, "space"),
        P("shot", "space", None),
        P("shot", "space"),
        P("shot"),
        P("shot", "space", None, None),
        P("shot", "space", None, None),
        P("shot", None, "space", None, None),
        P("space", None, None),
    )
    return jax.shard_map(
        shards,
        mesh=mesh,
        in_specs=placed,
        out_specs=(P("shot", "space", None, None), P("space", "shot", None)),
        check_vma=False,
    )
```
